512 devices in a mesh: tomo: 32 (over z, core), ref: 16 (over y, x).
Axes of the slice: x: 4, y: 4, z: 16, core: 2. Of those that a mesh axis runs over, the one named last changes fastest.
Arguments:
- particles: bfloat16 [1024, 64, 4096], P('tomo', 'ref'), may hold values from -6 to 6
- counts: int32 [32], P('tomo'), may hold values from 24 to 32, as said below
- block_of: int32 [1024], P('tomo'), may hold values from 0 to 31, as said below
- ref_index: int32 [1024], P('tomo'), may hold values from 0 to 7
- references: bfloat16 [256, 64, 2, 4096], P('tomo', None, None, 'ref'), may hold values from -6 to 6
- spectral_weight: float32 [64, 4096], P(None, 'ref'), may hold values from 0.1 to 1
Outputs:
- scores: float32 [1024], P('tomo')
- reconstruction: float32 [256, 64, 2, 4096], P('tomo', None, None, 'ref')
The draws below stay inside these ranges and needn't reach their ends.
Inputs may be any that keep to these rules, and one draw needn't show every extreme that they name: The live particles of tomogram t are its first counts[t] rows; some tomogram has all 32 live. `block_of`: of the 32 rows of one tomogram at most 2 are assigned to one block, and in every draw some block receives exactly 2 live particles from every tomogram.
All inputs are finite; a program needn't handle non-finite values.
Results may differ from the reference program's by a relative error of at most 0.0053.
Values may be sent and summed in bfloat16 or wider, within the bound.
No kernel may reach another device: no remote copies, remote signals or barrier semaphores. Data moves between devices by JAX's collectives and lax.ppermute only.
A program may use at most 128 MiB of HBM per device.

```python
import math
import jax
import jax.numpy as jnp
from jax import lax

BOX = 64
P_DEV = 32
REF_BLK = 8
TOMOGRAMS = 32
PARTICLES = 1024
REFS = 256


def routing(key):
    tomograms = TOMOGRAMS
    capacity = max(2, 2 * P_DEV // tomograms)
    slot_total = tomograms * capacity
    subkeys = jax.random.split(key, 6)
    lowest = max(capacity, 3 * P_DEV // 4)
    counts = jax.random.randint(subkeys[0], (tomograms,), lowest, P_DEV + 1)
    counts = counts.at[jax.random.randint(subkeys[1], (), 0, tomograms)].set(P_DEV)
    full_block = jax.random.randint(subkeys[2], (), 0, tomograms)
    favour = jax.random.randint(subkeys[3], (tomograms,), 0, 4)
    slot_owner = jnp.arange(slot_total, dtype=jnp.int32) // capacity
    base_draw = jax.random.randint(subkeys[4], (tomograms, slot_total), 0, 4096)
    priority = base_draw + favour[slot_owner] * 4096 + (slot_owner == full_block).astype(jnp.int32) * 65536
    priority = priority * slot_total + jnp.arange(slot_total, dtype=jnp.int32)[None, :]
    top_values, picked = lax.top_k(priority, P_DEV)
    chosen = picked // capacity
    row_ids = jnp.arange(P_DEV, dtype=jnp.int32)
    shuffle = jax.random.randint(subkeys[5], (tomograms, P_DEV), 0, 4096)
    order_key = jnp.where(row_ids[None, :] < counts[:, None], shuffle * P_DEV + row_ids[None, :], 4096 * P_DEV + row_ids[None, :])
    row_order = jnp.argsort(order_key, axis=1, stable=True)
    targets = jnp.take_along_axis(chosen, row_order, axis=1)
    return (counts.astype(jnp.int32), targets.reshape(-1).astype(jnp.int32))


def draw_counts(key, part):
    counts, targets = routing(key)
    return counts


def draw_block_of(key, part):
    counts, targets = routing(key)
    return targets


def set_ends(array, stream_key, least, top_value):
    dims = array.shape
    spot = [jax.random.randint(jax.random.fold_in(stream_key, axis), (), 0, dims[axis]) for axis in range(len(dims))]
    array = array.at[tuple(spot)].set(least)
    longest = dims.index(max(dims))
    spot[longest] = (spot[longest] + 1) % dims[longest]
    return array.at[tuple(spot)].set(top_value)


def steps_of(own_key, shape, cuts, smallest, top_value):
    gain = 1.0
    for dim, blocks in cuts:
        steps = jax.random.uniform(jax.random.fold_in(jax.random.fold_in(own_key, 6), dim), (blocks,), jnp.float32, smallest / len(cuts), top_value / len(cuts))
        gain = gain * jnp.repeat(jnp.exp(steps), shape[dim] // blocks).reshape((-1,) + (1,) * (len(shape) - 1 - dim))
    return gain


def gaussian(own_key, dims, deviation, most, pieces=(), kind=jnp.bfloat16):
    factor_of = steps_of(own_key, dims, pieces, -0.22, 0.18) if pieces else 1.0
    drawn = jax.random.normal(own_key, dims, jnp.float32) * deviation * factor_of
    return jnp.minimum(jnp.maximum(drawn, -most), most).astype(kind)


def setup_inputs(seed: int = 0) -> dict:
    splits = jax.random.split(jax.random.key(seed), 7)
    return {
        "particles": gaussian(splits[0], (PARTICLES, BOX, BOX * BOX), 1.0, 6.0, ((0, 32), (1, 16))),
        "counts": draw_counts(jax.random.fold_in(splits[6], 71), 0),
        "block_of": draw_block_of(jax.random.fold_in(splits[6], 71), 0),
        "ref_index": set_ends(jax.random.randint(splits[3], (PARTICLES,), 0, REF_BLK), jax.random.fold_in(splits[3], 1), 0, REF_BLK - 1).astype(jnp.int32),
        "references": gaussian(splits[4], (REFS, BOX, 2, BOX * BOX), 1.0, 6.0, ((0, 32), (3, 16))),
        "spectral_weight": jnp.clip(jnp.exp(math.log(1.0) - 2.3025851 * jax.random.uniform(splits[5], (BOX, BOX * BOX), jnp.float32) ** steps_of(splits[5], (BOX, BOX * BOX), ((1, 16),), -0.2, 0.2)), 0.1, 1.0),
    }


def spectrum_of(volume):
    values = volume.astype(jnp.float32).reshape(BOX, BOX, BOX)
    planes = jnp.fft.fft2(values, axes=(1, 2))
    plane_re = jnp.real(planes).astype(jnp.bfloat16)
    plane_im = jnp.imag(planes).astype(jnp.bfloat16)
    plane_re, plane_im = lax.optimization_barrier((plane_re, plane_im))
    rounded = lax.complex(plane_re.astype(jnp.float32), plane_im.astype(jnp.float32))
    depth_spectrum = jnp.fft.fft(rounded, axis=0)
    stacked = jnp.stack([jnp.real(depth_spectrum), jnp.imag(depth_spectrum)], axis=1)
    return stacked.reshape(BOX, 2, BOX * BOX).astype(jnp.bfloat16)

def reference(particles, counts, block_of, ref_index, references, spectral_weight):
    weight_cells = spectral_weight[:, None, :]
    score_scale = float(BOX) ** 1.5
    cell_total = float(BOX) ** 3

    def visit(reconstruction, inputs):
        volume, block_id, within, position = inputs
        spectrum_bf = spectrum_of(volume)
        spectrum_bf = lax.optimization_barrier(spectrum_bf)
        spectrum = spectrum_bf.astype(jnp.float32)
        target = (block_id * REF_BLK + within).astype(jnp.int32)
        weighted_ref = (weight_cells * references[target].astype(jnp.float32)).astype(jnp.bfloat16)
        weighted_ref = lax.optimization_barrier(weighted_ref)
        matched = jnp.sum(spectrum * weighted_ref.astype(jnp.float32))
        energy = jnp.sum(weight_cells * spectrum * spectrum)
        particle_norm = jnp.sqrt(energy / cell_total + 1e-05)
        is_live = (position % P_DEV < counts[position // P_DEV]).astype(jnp.float32)
        particle_score = is_live * matched / (score_scale * particle_norm)
        insertion = (is_live * jax.nn.sigmoid(particle_score) / particle_norm).astype(jnp.bfloat16)
        insertion = lax.optimization_barrier(insertion)
        reconstruction = reconstruction.at[target].add(insertion.astype(jnp.float32) * spectrum)
        return (reconstruction, particle_score)
    positions = jnp.arange(PARTICLES, dtype=jnp.int32)
    empty_recon = jnp.zeros((REFS, BOX, 2, BOX * BOX), jnp.float32)
    reconstruction, all_scores = lax.scan(visit, empty_recon, (particles, block_of, ref_index, positions))
    return (all_scores, reconstruction)
```

```python
import numpy as np

import jax
import jax.numpy as jnp
import ml_dtypes
from jax import lax
from jax.experimental import pallas as pl
from jax.experimental.pallas import tpu as pltpu
from jax.sharding import PartitionSpec as P

BOX = 64
HALF = 32
KY_DEV = 4
f32 = jnp.float32
bf16 = jnp.bfloat16


def split_hi_lo(table):
    high = table.astype(np.float32).astype(ml_dtypes.bfloat16)
    low = (table - high.astype(np.float64)).astype(np.float32).astype(ml_dtypes.bfloat16)
    return high, low


def angles(a, b):
    return 2.0 * np.pi / BOX * (np.outer(a, b) % BOX)


def x_table():
    x = np.arange(BOX)
    phase = angles(x, np.arange(HALF))
    real, imag = np.cos(phase), -np.sin(phase)
    imag[:, 0] = np.cos(np.pi * x)
    one = np.concatenate([real, imag, imag, -real], axis=1)
    table = np.zeros((2, BOX, 2, 4 * HALF))
    table[0, :, 0], table[1, :, 1] = one, one
    return np.concatenate(split_hi_lo(table.reshape(2 * BOX, 8 * HALF)), axis=0)


def y_table():
    rows = np.arange(BOX)
    ky = KY_DEV * (rows % 16) + rows // 16
    y = np.concatenate([np.arange(0, BOX, 2), np.arange(1, BOX, 2)])
    phase = angles(ky, y)
    high, low = split_hi_lo(np.concatenate([np.cos(phase), np.sin(phase)], axis=1))
    return np.concatenate(
        [
            np.concatenate([high, high], axis=1),
            np.concatenate([low, np.zeros_like(low)], axis=1),
        ],
        axis=0,
    )


def z_table():
    phase = angles(np.arange(BOX), np.arange(BOX))
    table = np.zeros((2, BOX, BOX, 2))
    table[0, :, :, 0], table[0, :, :, 1] = np.cos(phase), np.sin(phase)
    table[1, :, :, 0], table[1, :, :, 1] = -np.sin(phase), np.cos(phase)
    return np.concatenate(split_hi_lo(table.reshape(2 * BOX, 2 * BOX)), axis=1)


def unfold_tables():
    own, mirror = np.zeros((KY_DEV, HALF, KY_DEV, BOX)), np.zeros((KY_DEV, HALF, KY_DEV, BOX))
    own_turned, mirror_turned = np.zeros_like(own), np.zeros_like(own)
    for kyl in range(KY_DEV):
        to = (KY_DEV - kyl) % KY_DEV
        own[kyl, 0, kyl, 0] = mirror[kyl, 0, to, 0] = 0.5
        own_turned[kyl, 0, kyl, HALF], mirror_turned[kyl, 0, to, HALF] = 0.5, -0.5
        for kx in range(1, HALF):
            own[kyl, kx, kyl, kx] = mirror[kyl, kx, to, BOX - kx] = 1.0
    stacked = np.concatenate([own, own, mirror, own_turned, own_turned, mirror_turned], axis=0)
    reverse = np.zeros((2, BOX, 2, BOX))
    for kz in range(BOX):
        reverse[0, kz, 0, -kz % BOX], reverse[1, kz, 1, -kz % BOX] = 1.0, -1.0
    return (
        stacked.reshape(6 * 2 * BOX, 4 * BOX).astype(ml_dtypes.bfloat16),
        reverse.reshape(2 * BOX, 2 * BOX).astype(ml_dtypes.bfloat16),
    )


def params():
    return pltpu.CompilerParams(vmem_limit_bytes=40 * 2**20)


def dot(a, b):
    return jnp.dot(a, b, preferred_element_type=f32)


def planes_kernel(x_ref, wx_ref, ty_ref, out_ref, rows_buf, turn_buf):
    lane = lax.broadcasted_iota(jnp.int32, (1, 128), 1)
    low_half = lane < 64
    even = lane % 64 < 32
    for pair in range(x_ref.shape[0] // 2):
        for e in range(2):
            volume = x_ref[2 * pair + e].astype(f32)
            for yt in range(32):
                rows_buf[256 * e + 8 * yt : 256 * e + 8 * yt + 4, :] = volume[:, yt * 128 : (yt + 1) * 128]
            x = jnp.concatenate(
                [rows_buf[pl.ds(256 * e + zl, 32, stride=8), :] for zl in range(4)], axis=0
            ).astype(bf16)
            along = dot(jnp.concatenate([x, x], axis=1), wx_ref[...])
            tiles = []
            for zp in range(2):
                first, second = [], []
                for h in range(2):
                    a = along[64 * zp : 64 * zp + 32, 128 * h : 128 * h + 128]
                    b = along[64 * zp + 32 : 64 * zp + 64, 128 * h : 128 * h + 128]
                    first.append(jnp.where(low_half, a, pltpu.roll(b, 64, 1)))
                    second.append(jnp.where(low_half, pltpu.roll(a, 64, 1), b))
                tiles.append(jnp.concatenate(first + second, axis=0))
            wide = jnp.concatenate(tiles, axis=1)
            high = wide.astype(bf16)
            low = (wide - high.astype(f32)).astype(bf16)
            full = dot(ty_ref[...], jnp.concatenate([high, low], axis=0))
            planes = full[:64] + full[64:]
            for zp in range(2):
                i0, i1, i2, i3 = (
                    planes[16 * k : 16 * k + 16, 128 * zp : 128 * zp + 128] for k in range(4)
                )
                p0 = jnp.where(low_half, i0, pltpu.roll(i2, 64, 1))
                p2 = jnp.where(low_half, pltpu.roll(i0, 64, 1), i2)
                p1 = jnp.where(low_half, i1, pltpu.roll(i3, 64, 1))
                p3 = jnp.where(low_half, pltpu.roll(i1, 64, 1), i3)
                turned = (
                    jnp.where(even, p0, pltpu.roll(p1, 32, 1)),
                    jnp.where(even, pltpu.roll(p0, 96, 1), p1),
                    jnp.where(even, p2, pltpu.roll(p3, 32, 1)),
                    jnp.where(even, pltpu.roll(p2, 96, 1), p3),
                )
                for g in range(4):
                    start = 128 * e + (4 * zp + g) * 16
                    turn_buf[start : start + 16, :] = turned[g]
        for j in range(16):
            both = [turn_buf[pl.ds(128 * e + j, 8, stride=16), :] for e in range(2)]
            out_ref[j, pair] = jnp.concatenate(both, axis=0).astype(bf16)


def half_planes(particles):
    rows = particles.shape[0]
    group = 4
    return pl.pallas_call(
        planes_kernel,
        grid=(rows // group,),
        in_specs=[
            pl.BlockSpec((group, 4, BOX * BOX), lambda i: (i, 0, 0)),
            pl.BlockSpec((256, 256), lambda i: (0, 0)),
            pl.BlockSpec((128, 256), lambda i: (0, 0)),
        ],
        out_specs=pl.BlockSpec((16, group // 2, 16, 128), lambda i: (0, i, 0, 0)),
        out_shape=jax.ShapeDtypeStruct((16, rows // 2, 16, 128), bf16),
        scratch_shapes=[pltpu.VMEM((512, 128), f32), pltpu.VMEM((256, 128), f32)],
        compiler_params=params(),
        name="half_planes",
    )(particles, jnp.asarray(x_table()), jnp.asarray(y_table()))


def depth_kernel(slot_ref, b_ref, td_ref, spec_ref, send_ref):
    slots = send_ref.shape[0]

    def clear(s, _):
        send_ref[s] = jnp.zeros((128, 128), bf16)
        return 0

    lax.fori_loop(0, slots, clear, 0)

    def step(pair, _):
        block = b_ref[:, pair].astype(f32)
        a = block[:, :8, :].reshape(128, 128)
        b = block[:, 8:, :].reshape(128, 128)
        pencils = jnp.concatenate([a, b], axis=1).astype(bf16)
        spectra = dot(td_ref[...], jnp.concatenate([pencils, pencils], axis=0)).astype(bf16)
        for e in range(2):
            one = spectra[:, 128 * e : 128 * e + 128]
            row = 2 * pair + e
            spec_ref[row] = one
            slot = slot_ref[row]

            @pl.when(slot < slots)
            def _():
                send_ref[slot] = one

        return 0

    lax.fori_loop(0, b_ref.shape[1], step, 0)


def half_spectra(slot_of, pencils, slots):
    rows = 2 * pencils.shape[1]
    vmem = pl.BlockSpec(memory_space=pltpu.VMEM)
    return pl.pallas_call(
        depth_kernel,
        in_specs=[pl.BlockSpec(memory_space=pltpu.SMEM), vmem, vmem],
        out_specs=[vmem, vmem],
        out_shape=[
            jax.ShapeDtypeStruct((rows, 128, 128), bf16),
            jax.ShapeDtypeStruct((slots, 128, 128), bf16),
        ],
        compiler_params=params(),
        name="half_spectra",
    )(slot_of, pencils, jnp.asarray(z_table()))


def match_kernel(index_ref, spec_ref, coef_ref, out_ref):
    group = spec_ref.shape[0]
    base = pl.program_id(0) * group
    for s in range(group):
        product = spec_ref[s].astype(f32) * coef_ref[index_ref[base + s]]
        out_ref[s : s + 1, :] = jnp.sum(product, axis=0, keepdims=True)


def match(index, spectra, coefficients):
    slots = spectra.shape[0]
    refs = coefficients.shape[0]
    group = min(8, slots)
    return pl.pallas_call(
        match_kernel,
        grid_spec=pltpu.PrefetchScalarGridSpec(
            num_scalar_prefetch=1,
            grid=(slots // group,),
            in_specs=[
                pl.BlockSpec((group, 128, 128), lambda i, _: (i, 0, 0)),
                pl.BlockSpec((refs, 128, 128), lambda i, _: (0, 0, 0)),
            ],
            out_specs=pl.BlockSpec((group, 128), lambda i, _: (i, 0)),
        ),
        out_shape=jax.ShapeDtypeStruct((slots, 128), f32),
        compiler_params=params(),
        name="match",
    )(index, spectra, coefficients)


def insert_kernel(index_ref, gain_ref, spec_ref, out_ref, sent_ref):
    group = spec_ref.shape[0]
    step = pl.program_id(0)

    @pl.when(step == 0)
    def _():
        out_ref[...] = jnp.zeros_like(out_ref)

    for s in range(group):
        slot = step * group + s
        out_ref[index_ref[slot]] += gain_ref[slot] * spec_ref[s].astype(f32)

    @pl.when(step == pl.num_programs(0) - 1)
    def _():
        sent_ref[...] = out_ref[...].astype(bf16)


def insert(index, gain, spectra, refs):
    slots = spectra.shape[0]
    group = min(8, slots)
    whole = pl.BlockSpec((refs, 128, 128), lambda i, *_: (0, 0, 0))
    return pl.pallas_call(
        insert_kernel,
        grid_spec=pltpu.PrefetchScalarGridSpec(
            num_scalar_prefetch=2,
            grid=(slots // group,),
            in_specs=[pl.BlockSpec((group, 128, 128), lambda i, *_: (i, 0, 0))],
            out_specs=[whole, whole],
        ),
        out_shape=[
            jax.ShapeDtypeStruct((refs, 128, 128), f32),
            jax.ShapeDtypeStruct((refs, 128, 128), bf16),
        ],
        compiler_params=params(),
        name="insert",
    )(index, gain, spectra)


def unfold_kernel(own_ref, near_ref, far_ref, q_ref, reverse_ref, out_ref):
    lane = lax.broadcasted_iota(jnp.int32, (1, 128), 1)
    own = own_ref[...]
    partner = jnp.where(lane < HALF, near_ref[...].astype(f32), far_ref[...].astype(f32)).astype(bf16)
    conjugate = dot(reverse_ref[...], partner)

    def turned(v):
        return jnp.concatenate([v[64:], -v[:64]], axis=0)

    high = own.astype(bf16).astype(f32)
    parts = [high, own - high, conjugate]
    parts = parts + [turned(v) for v in parts]
    full = dot(jnp.concatenate(parts, axis=1).astype(bf16), q_ref[...])
    for lt in range(2):
        for c in range(2):
            out_ref[pl.ds(2 * lt + c, 64, stride=4), :] = full[
                64 * c : 64 * c + 64, 128 * lt : 128 * lt + 128
            ]


def unfold(own, near, far):
    refs = own.shape[0]
    stacked, reverse = unfold_tables()
    one = pl.BlockSpec((None, 128, 128), lambda i: (i, 0, 0))
    packed = pl.pallas_call(
        unfold_kernel,
        grid=(refs,),
        in_specs=[
            one,
            one,
            one,
            pl.BlockSpec((768, 256), lambda i: (0, 0)),
            pl.BlockSpec((128, 128), lambda i: (0, 0)),
        ],
        out_specs=pl.BlockSpec((None, 256, 128), lambda i: (i, 0, 0)),
        out_shape=jax.ShapeDtypeStruct((refs, 256, 128), f32),
        compiler_params=params(),
        name="unfold",
    )(own, near, far, jnp.asarray(stacked), jnp.asarray(reverse))
    tiles = packed.reshape(refs, BOX, 2, 2, 128)
    return tiles.transpose(0, 1, 3, 2, 4).reshape(refs, BOX, 2, 256)


def to_far(values):
    return lax.ppermute(values, "ref", [(j, 15 - j) for j in range(16)])


def to_near(values):
    return lax.ppermute(values, "ref", [(j, -j % 16) for j in range(16)])


def mirrored(values, ky_axis):
    near = to_near(lax.slice_in_dim(values, 0, 1, axis=ky_axis))
    far = to_far(lax.slice_in_dim(values, 1, KY_DEV, axis=ky_axis))
    return jnp.concatenate([near, lax.rev(far, (ky_axis,))], axis=ky_axis)


def minus_index(values, axis):
    return jnp.roll(lax.rev(values, (axis,)), 1, axis)


def minus_kx(values):
    order = np.zeros((BOX, BOX), np.float32)
    for kx in range(BOX):
        order[-kx % BOX, kx] = 1.0
    return jnp.einsum(
        "...x,xk->...k", values, jnp.asarray(order, values.dtype), precision=lax.Precision.HIGHEST,
        preferred_element_type=f32,
    )


def folded_references(references, spectral_weight):
    refs = references.shape[0]
    weighted = (spectral_weight[None, :, None, :] * references.astype(f32)).astype(bf16)
    weighted = weighted.reshape(refs, BOX, 2, KY_DEV, BOX)
    other = minus_kx(minus_index(mirrored(weighted, 3), 1))
    weighted = weighted.astype(f32)
    real = weighted[:, :, 0] + other[:, :, 0]
    imag = weighted[:, :, 1] - other[:, :, 1]
    first = jnp.arange(HALF) == 0
    real_half = jnp.where(
        first, 0.5 * (real[..., :1] - imag[..., HALF : HALF + 1]), real[..., :HALF]
    )
    imag_half = jnp.where(
        first, 0.5 * (imag[..., :1] + real[..., HALF : HALF + 1]), imag[..., :HALF]
    )
    both = jnp.stack([real_half, imag_half], axis=1)
    return both.reshape(refs, 128, 128)


def half_energy(spectra, spectral_weight):
    rows = spectra.shape[0]
    weight = spectral_weight.reshape(BOX, KY_DEV, BOX)
    fold = weight + minus_kx(minus_index(mirrored(weight, 1), 0))
    ends_sum = 0.25 * (fold[..., :1] + fold[..., HALF : HALF + 1])
    ends_difference = 0.25 * (fold[..., 0] - fold[..., HALF])
    fold = jnp.where(jnp.arange(HALF) == 0, ends_sum, fold[..., :HALF]).reshape(BOX, 128)
    values = spectra.astype(f32).reshape(rows, 2, BOX, 128)
    energy = jnp.sum(values * values * fold[None, None], axis=(1, 2, 3))
    pick = np.zeros((128, KY_DEV), np.float32)
    for kyl in range(KY_DEV):
        pick[kyl * HALF, kyl] = 1.0
    ends = jnp.einsum(
        "nrl,lk->nrk", spectra, jnp.asarray(pick, bf16), preferred_element_type=f32
    ).reshape(rows, 2, BOX, KY_DEV)
    other = minus_index(mirrored(ends, 3), 2)
    cross = ends[:, 0] * other[:, 0] - ends[:, 1] * other[:, 1]
    return energy + jnp.sum(cross * ends_difference[None], axis=(1, 2))


def body(particles, counts, block_of, ref_index, references, spectral_weight):
    tomograms = lax.axis_size("tomo")
    rows = particles.shape[0]
    slots = 2 * tomograms
    refs = references.shape[0]
    positions = jnp.arange(rows, dtype=jnp.int32)

    is_live = positions < counts[0]
    same = (block_of[:, None] == block_of[None, :]) & is_live[:, None]
    before = positions[:, None] < positions[None, :]
    rank = jnp.sum((same & before).astype(jnp.int32), axis=0)
    slot_of = jnp.where(is_live, 2 * block_of + rank, slots)

    planes = half_planes(particles)
    pencils = lax.all_to_all(planes, "ref", split_axis=0, concat_axis=0, tiled=True)
    spectra, outgoing = half_spectra(slot_of, pencils, slots)
    arrived = lax.all_to_all(outgoing, "tomo", split_axis=0, concat_axis=0, tiled=True)

    coefficients = folded_references(references, spectral_weight)
    energy = jnp.sum(lax.all_gather(half_energy(spectra, spectral_weight), "ref"), axis=0)
    routing = jnp.where(is_live, block_of * refs + ref_index, -1)
    all_routing = lax.all_gather(routing, "tomo")
    all_energy = lax.all_gather(energy, "tomo")
    own_block = lax.axis_index("tomo")
    mine = (all_routing >= 0) & (all_routing // refs == own_block)
    order = jnp.cumsum(mine.astype(jnp.int32), axis=1)
    chosen = mine[:, None, :] & (order[:, None, :] == jnp.arange(1, 3, dtype=jnp.int32)[None, :, None])
    filled = jnp.any(chosen, axis=2).reshape(slots)
    slot_index = jnp.sum(jnp.where(chosen, all_routing[:, None, :] % refs, 0), axis=2).reshape(slots)
    slot_energy = jnp.sum(jnp.where(chosen, all_energy[:, None, :], 0.0), axis=2).reshape(slots)
    particle_norm = jnp.sqrt(slot_energy / float(BOX) ** 3 + 1e-05)

    partial = jnp.sum(match(slot_index, arrived, coefficients), axis=1)
    spread = jnp.broadcast_to(partial[None, None, :], (16, 1, slots))
    gathered = lax.all_to_all(spread, "ref", split_axis=0, concat_axis=0, tiled=True)
    matched = jnp.sum(gathered, axis=(0, 1))
    slot_scores = jnp.where(filled, matched / (float(BOX) ** 1.5 * particle_norm), 0.0)
    gain = jnp.where(filled, jax.nn.sigmoid(slot_scores) / particle_norm, 0.0)
    gain = gain.astype(bf16).astype(f32)

    returned = lax.all_to_all(
        slot_scores.reshape(tomograms, 1, 2), "tomo", split_axis=0, concat_axis=0, tiled=True
    )
    half, half_sent = insert(slot_index, gain, arrived, refs)
    reconstruction = unfold(half, to_near(half_sent), to_far(half_sent))

    slot_match = slot_of[None, :] == jnp.arange(slots, dtype=jnp.int32)[:, None]
    row_scores = jnp.sum(jnp.where(slot_match, returned.reshape(slots)[:, None], 0.0), axis=0)
    return (row_scores, reconstruction)


def solution(mesh):
    placed = (
        P("tomo", "ref", None),
        P("tomo"),
        P("tomo"),
        P("tomo"),
        P("tomo", None, None, "ref"),
        P(None, "ref"),
    )
    return jax.shard_map(
        body,
        mesh=mesh,
        in_specs=placed,
        out_specs=(P("tomo"), P("tomo", None, None, "ref")),
        check_vma=False,
    )
```

```python
import numpy as np

import jax
import jax.numpy as jnp
import ml_dtypes
from jax import lax
from jax.experimental import pallas as pl
from jax.experimental.pallas import tpu as pltpu
from jax.sharding import PartitionSpec as P

BOX = 64
HALF = 32
KY_DEV = 4
f32 = jnp.float32
bf16 = jnp.bfloat16


def split_hi_lo(table):
    high = table.astype(np.float32).astype(ml_dtypes.bfloat16)
    low = (table - high.astype(np.float64)).astype(np.float32).astype(ml_dtypes.bfloat16)
    return high, low


def angles(a, b):
    return 2.0 * np.pi / BOX * (np.outer(a, b) % BOX)


def x_table():
    x = np.arange(BOX)
    phase = angles(x, np.arange(HALF))
    real, imag = np.cos(phase), -np.sin(phase)
    imag[:, 0] = np.cos(np.pi * x)
    one = np.concatenate([real, imag, imag, -real], axis=1)
    table = np.zeros((2, BOX, 2, 4 * HALF))
    table[0, :, 0], table[1, :, 1] = one, one
    return np.concatenate(split_hi_lo(table.reshape(2 * BOX, 8 * HALF)), axis=0)


def y_table():
    rows = np.arange(BOX)
    ky = KY_DEV * (rows % 16) + rows // 16
    y = np.concatenate([np.arange(0, BOX, 2), np.arange(1, BOX, 2)])
    cosine, sine = np.cos(angles(ky, y)), np.sin(angles(ky, y))
    zero = np.zeros_like(cosine)
    plain = np.concatenate([cosine, sine], axis=1)
    lower = ky[:, None] < 32
    packed = ky[:, None] % 32 == 0
    real = np.where(lower, np.concatenate([cosine, zero], 1), np.concatenate([zero, cosine], 1))
    imag = np.where(lower, np.concatenate([zero, sine], 1), np.concatenate([-sine, zero], 1))
    real, imag = np.where(packed, plain, real), np.where(packed, plain, imag)
    high, low = split_hi_lo(np.concatenate([plain, real, imag], axis=0))
    return np.concatenate(
        [
            np.concatenate([high, high], axis=1),
            np.concatenate([low, np.zeros_like(low)], axis=1),
        ],
        axis=0,
    )


def z_table():
    phase = angles(np.arange(BOX), np.arange(BOX))
    table = np.zeros((2, BOX, BOX, 2))
    table[0, :, :, 0], table[0, :, :, 1] = np.cos(phase), np.sin(phase)
    table[1, :, :, 0], table[1, :, :, 1] = -np.sin(phase), np.cos(phase)
    return np.concatenate(split_hi_lo(table.reshape(2 * BOX, 2 * BOX)), axis=1)


def reverse_table():
    reverse = np.zeros((2, BOX, 2, BOX))
    for kz in range(BOX):
        reverse[0, kz, 0, -kz % BOX], reverse[1, kz, 1, -kz % BOX] = 1.0, -1.0
    return reverse.reshape(2 * BOX, 2 * BOX).astype(ml_dtypes.bfloat16)


def unfold_table(j):
    own, mirror = np.zeros((KY_DEV, HALF, KY_DEV, BOX)), np.zeros((KY_DEV, HALF, KY_DEV, BOX))
    own_turned, mirror_turned = np.zeros_like(own), np.zeros_like(own)
    here, there = (0, HALF) if j < 8 else (HALF, 0)
    for kyl in range(KY_DEV):
        to = (KY_DEV - kyl) % KY_DEV
        if kyl == 0 and j % 8 == 0:
            own[0, 0, 0, 0] = mirror[0, 0, 0, 0] = 0.5
            own_turned[0, 0, 0, HALF], mirror_turned[0, 0, 0, HALF] = 0.5, -0.5
        else:
            own[kyl, 0, kyl, here] = mirror[kyl, 0, to, there] = 1.0
        for kx in range(1, HALF):
            own[kyl, kx, kyl, kx] = mirror[kyl, kx, to, BOX - kx] = 1.0
    stacked = np.concatenate([own, own, mirror, own_turned, own_turned, mirror_turned], axis=0)
    return stacked.reshape(6 * 2 * BOX, 4 * BOX).astype(ml_dtypes.bfloat16)


def table_of_device():
    j = lax.axis_index("ref")
    return jnp.where(j % 8 == 0, 2, 0) + jnp.where(j < 8, 0, 1)


def unfold_tables():
    return np.concatenate([unfold_table(j) for j in (1, 9, 0, 8)], axis=0)


def params():
    return pltpu.CompilerParams(vmem_limit_bytes=40 * 2**20)


def cost(microseconds):
    return pl.CostEstimate(
        flops=0, bytes_accessed=int(microseconds * 3.0e6), transcendentals=0
    )


def dot(a, b):
    return jnp.dot(a, b, preferred_element_type=f32)


def planes_kernel(x_ref, table_ref, out_ref, rows_buf, turn_buf):
    lane = lax.broadcasted_iota(jnp.int32, (1, 128), 1)
    low_half = lane < 64
    even = lane % 64 < 32
    wide_lane = lax.broadcasted_iota(jnp.int32, (1, 256), 1) % 64
    for pair in range(x_ref.shape[0] // 2):
        for e in range(2):
            volume = x_ref[2 * pair + e].astype(f32)
            for yt in range(32):
                rows_buf[256 * e + 8 * yt : 256 * e + 8 * yt + 4, :] = volume[:, yt * 128 : (yt + 1) * 128]
            x = jnp.concatenate(
                [rows_buf[pl.ds(256 * e + zl, 32, stride=8), :] for zl in range(4)], axis=0
            ).astype(bf16)
            along = dot(jnp.concatenate([x, x], axis=1), table_ref[:256])
            tiles = []
            for zp in range(2):
                first, second = [], []
                for h in range(2):
                    a = along[64 * zp : 64 * zp + 32, 128 * h : 128 * h + 128]
                    b = along[64 * zp + 32 : 64 * zp + 64, 128 * h : 128 * h + 128]
                    first.append(jnp.where(low_half, a, pltpu.roll(b, 64, 1)))
                    second.append(jnp.where(low_half, pltpu.roll(a, 64, 1), b))
                tiles.append(jnp.concatenate(first + second, axis=0))
            wide = jnp.concatenate(tiles, axis=1)
            high = wide.astype(bf16)
            low = (wide - high.astype(f32)).astype(bf16)
            full = dot(table_ref[256:], jnp.concatenate([high, low], axis=0))
            full = full[:192] + full[192:]
            planes = jnp.where(wide_lane == 0, full[64:128], full[:64])
            planes = jnp.where(wide_lane == 32, full[128:], planes)
            for zp in range(2):
                i0, i1, i2, i3 = (
                    planes[16 * k : 16 * k + 16, 128 * zp : 128 * zp + 128] for k in range(4)
                )
                p0 = jnp.where(low_half, i0, pltpu.roll(i2, 64, 1))
                p2 = jnp.where(low_half, pltpu.roll(i0, 64, 1), i2)
                p1 = jnp.where(low_half, i1, pltpu.roll(i3, 64, 1))
                p3 = jnp.where(low_half, pltpu.roll(i1, 64, 1), i3)
                turned = (
                    jnp.where(even, p0, pltpu.roll(p1, 32, 1)),
                    jnp.where(even, pltpu.roll(p0, 96, 1), p1),
                    jnp.where(even, p2, pltpu.roll(p3, 32, 1)),
                    jnp.where(even, pltpu.roll(p2, 96, 1), p3),
                )
                for g in range(4):
                    start = 128 * e + (4 * zp + g) * 16
                    turn_buf[start : start + 16, :] = turned[g]
        for j in range(16):
            both = [turn_buf[pl.ds(128 * e + j, 8, stride=16), :] for e in range(2)]
            out_ref[j, pair] = jnp.concatenate(both, axis=0).astype(bf16)


def half_planes(particles):
    rows = particles.shape[0]
    group = 4
    return pl.pallas_call(
        planes_kernel,
        grid=(rows // group,),
        in_specs=[
            pl.BlockSpec((group, 4, BOX * BOX), lambda i: (i, 0, 0)),
            pl.BlockSpec((640, 256), lambda i: (0, 0)),
        ],
        out_specs=pl.BlockSpec((16, group // 2, 16, 128), lambda i: (0, i, 0, 0)),
        out_shape=jax.ShapeDtypeStruct((16, rows // 2, 16, 128), bf16),
        scratch_shapes=[pltpu.VMEM((512, 128), f32), pltpu.VMEM((256, 128), f32)],
        compiler_params=params(),
        cost_estimate=cost(8.0),
        name="half_planes",
    )(particles, jnp.asarray(np.concatenate([x_table(), y_table()], axis=0)))


def depth_kernel(slot_ref, index_ref, b_ref, table_ref, weight_ref, send_ref, extra_buf):
    slots = extra_buf.shape[0]
    tomograms = slots // 2
    line = lax.broadcasted_iota(jnp.int32, (8, 128), 0)

    def clear(t, _):
        send_ref[pl.ds(17 * t, 16)] = jnp.zeros((16, 16, 128), bf16)
        extra_buf[pl.ds(2 * t, 2)] = jnp.zeros((2, 8, 128), f32)
        return 0

    lax.fori_loop(0, tomograms, clear, 0)

    def step(pair, _):
        block = b_ref[:, pair].astype(f32)
        a = block[:, :8, :].reshape(128, 128)
        b = block[:, 8:, :].reshape(128, 128)
        pencils = jnp.concatenate([a, b], axis=1).astype(bf16)
        spectra = dot(table_ref[:128], jnp.concatenate([pencils, pencils], axis=0)).astype(bf16)
        turned = dot(table_ref[128:, :128], spectra)
        for e in range(2):
            one = spectra[:, 128 * e : 128 * e + 128]
            value = one.astype(f32)
            terms = value * weight_ref[0] + turned[:, 128 * e : 128 * e + 128] * weight_ref[1]
            energy = jnp.sum(value * terms, axis=0, keepdims=True)
            high = energy.astype(bf16).astype(f32)
            middle = (energy - high).astype(bf16).astype(f32)
            low = energy - high - middle
            row = 2 * pair + e
            slot = slot_ref[row]
            number = (index_ref[row] + 1).astype(f32)
            extra = jnp.where(line == 0, high, jnp.where(line == 1, middle, low))
            extra = jnp.where(line == 3, number, extra)

            @pl.when(slot < slots)
            def _():
                send_ref[pl.ds(17 * (slot // 2) + 8 * (slot % 2), 8)] = one.reshape(8, 16, 128)
                extra_buf[slot] = extra

        return 0

    lax.fori_loop(0, b_ref.shape[1], step, 0)

    def finish(t, _):
        both = jnp.concatenate([extra_buf[2 * t], extra_buf[2 * t + 1]], axis=0)
        send_ref[17 * t + 16] = both.astype(bf16)
        return 0

    lax.fori_loop(0, tomograms, finish, 0)


def half_spectra(slot_of, ref_index, pencils, weights, slots):
    vmem = pl.BlockSpec(memory_space=pltpu.VMEM)
    smem = pl.BlockSpec(memory_space=pltpu.SMEM)
    reverse = np.concatenate([reverse_table(), np.zeros_like(reverse_table())], axis=1)
    return pl.pallas_call(
        depth_kernel,
        in_specs=[smem, smem, vmem, vmem, vmem],
        out_specs=vmem,
        out_shape=jax.ShapeDtypeStruct((slots // 2 * 17, 16, 128), bf16),
        scratch_shapes=[pltpu.VMEM((slots, 8, 128), f32)],
        compiler_params=params(),
        cost_estimate=cost(4.0),
        name="half_spectra",
    )(slot_of, ref_index, pencils, jnp.asarray(np.concatenate([z_table(), reverse])), weights)


def match_kernel(index_ref, spec_ref, coef_ref, out_ref):
    group = spec_ref.shape[0] // 17
    base = pl.program_id(0) * 2 * group
    for t in range(group):
        extra = spec_ref[17 * t + 16].astype(f32)
        for k in range(2):
            s = 2 * t + k
            value = spec_ref[17 * t + 8 * k : 17 * t + 8 * k + 8].reshape(128, 128).astype(f32)
            product = value * coef_ref[index_ref[base + s]]
            out_ref[0, s : s + 1, :] = jnp.sum(product, axis=0, keepdims=True)
            parts = extra[8 * k : 8 * k + 3]
            out_ref[1, s : s + 1, :] = jnp.sum(parts, axis=0, keepdims=True)


def match(index, arrived, coefficients):
    slots = index.shape[0]
    refs = coefficients.shape[0]
    group = min(4, slots // 2)
    return pl.pallas_call(
        match_kernel,
        grid_spec=pltpu.PrefetchScalarGridSpec(
            num_scalar_prefetch=1,
            grid=(slots // 2 // group,),
            in_specs=[
                pl.BlockSpec((17 * group, 16, 128), lambda i, _: (i, 0, 0)),
                pl.BlockSpec((refs, 128, 128), lambda i, _: (0, 0, 0)),
            ],
            out_specs=pl.BlockSpec((2, 2 * group, 128), lambda i, _: (0, i, 0)),
        ),
        out_shape=jax.ShapeDtypeStruct((2, slots, 128), f32),
        compiler_params=params(),
        cost_estimate=cost(2.0),
        name="match",
    )(index, arrived, coefficients)


def insert_kernel(index_ref, gain_ref, spec_ref, out_ref, sent_ref):
    group = spec_ref.shape[0] // 17
    step = pl.program_id(0)

    @pl.when(step == 0)
    def _():
        out_ref[...] = jnp.zeros_like(out_ref)

    for t in range(group):
        for k in range(2):
            slot = step * 2 * group + 2 * t + k
            value = spec_ref[17 * t + 8 * k : 17 * t + 8 * k + 8].reshape(128, 128).astype(f32)
            out_ref[index_ref[slot]] += gain_ref[slot] * value

    @pl.when(step == pl.num_programs(0) - 1)
    def _():
        sent_ref[...] = out_ref[...].astype(bf16)


def insert(index, gain, arrived, refs):
    slots = index.shape[0]
    group = min(4, slots // 2)
    whole = pl.BlockSpec((refs, 128, 128), lambda i, *_: (0, 0, 0))
    return pl.pallas_call(
        insert_kernel,
        grid_spec=pltpu.PrefetchScalarGridSpec(
            num_scalar_prefetch=2,
            grid=(slots // 2 // group,),
            in_specs=[pl.BlockSpec((17 * group, 16, 128), lambda i, *_: (i, 0, 0))],
            out_specs=[whole, whole],
        ),
        out_shape=[
            jax.ShapeDtypeStruct((refs, 128, 128), f32),
            jax.ShapeDtypeStruct((refs, 128, 128), bf16),
        ],
        compiler_params=params(),
        cost_estimate=cost(2.0),
        name="insert",
    )(index, gain, arrived)


def unfold_kernel(kind_ref, own_ref, near_ref, far_ref, q_ref, reverse_ref, out_ref):
    lane = lax.broadcasted_iota(jnp.int32, (1, 128), 1)
    own = own_ref[...]
    partner = jnp.where(lane < HALF, near_ref[...].astype(f32), far_ref[...].astype(f32)).astype(bf16)
    conjugate = dot(reverse_ref[...], partner)

    def turned(v):
        return jnp.concatenate([v[64:], -v[:64]], axis=0)

    high = own.astype(bf16).astype(f32)
    parts = [high, own - high, conjugate]
    parts = parts + [turned(v) for v in parts]
    full = dot(jnp.concatenate(parts, axis=1).astype(bf16), q_ref[...])
    for lt in range(2):
        for c in range(2):
            out_ref[pl.ds(2 * lt + c, 64, stride=4), :] = full[
                64 * c : 64 * c + 64, 128 * lt : 128 * lt + 128
            ]


def unfold(own, near, far):
    refs = own.shape[0]
    one = pl.BlockSpec((None, 128, 128), lambda i, _: (i, 0, 0))
    packed = pl.pallas_call(
        unfold_kernel,
        grid_spec=pltpu.PrefetchScalarGridSpec(
            num_scalar_prefetch=1,
            grid=(refs,),
            in_specs=[
                one,
                one,
                one,
                pl.BlockSpec((768, 256), lambda i, kind: (kind[0], 0)),
                pl.BlockSpec((128, 128), lambda i, _: (0, 0)),
            ],
            out_specs=pl.BlockSpec((None, 256, 128), lambda i, _: (i, 0, 0)),
        ),
        out_shape=jax.ShapeDtypeStruct((refs, 256, 128), f32),
        compiler_params=params(),
        cost_estimate=cost(5.0),
        name="unfold",
    )(
        table_of_device().astype(jnp.int32).reshape(1),
        own,
        near,
        far,
        jnp.asarray(unfold_tables()),
        jnp.asarray(reverse_table()),
    )
    tiles = packed.reshape(refs, BOX, 2, 2, 128)
    return tiles.transpose(0, 1, 3, 2, 4).reshape(refs, BOX, 2, 256)


def to_far(values):
    return lax.ppermute(values, "ref", [(j, 15 - j) for j in range(16)])


def to_near(values):
    return lax.ppermute(values, "ref", [(j, -j % 16) for j in range(16)])


def mirrored(values, ky_axis):
    near = to_near(lax.slice_in_dim(values, 0, 1, axis=ky_axis))
    far = to_far(lax.slice_in_dim(values, 1, KY_DEV, axis=ky_axis))
    return jnp.concatenate([near, lax.rev(far, (ky_axis,))], axis=ky_axis)


def minus_index(values, axis):
    return jnp.roll(lax.rev(values, (axis,)), 1, axis)


def minus_kx(values):
    order = np.zeros((BOX, BOX), np.float32)
    for kx in range(BOX):
        order[-kx % BOX, kx] = 1.0
    return jnp.einsum(
        "...x,xk->...k", values, jnp.asarray(order, values.dtype), precision=lax.Precision.HIGHEST,
        preferred_element_type=f32,
    )


def column_kinds():
    j = lax.axis_index("ref")
    return j < 8, (j % 8 == 0) & (jnp.arange(KY_DEV) == 0)


def folded_references(references, spectral_weight):
    refs = references.shape[0]
    weighted = (spectral_weight[None, :, None, :] * references.astype(f32)).astype(bf16)
    weighted = weighted.reshape(refs, BOX, 2, KY_DEV, BOX)
    other = minus_kx(minus_index(mirrored(weighted, 3), 1))
    weighted = weighted.astype(f32)
    real = weighted[:, :, 0] + other[:, :, 0]
    imag = weighted[:, :, 1] - other[:, :, 1]
    real_0, real_32 = real[..., 0], real[..., HALF]
    imag_0, imag_32 = imag[..., 0], imag[..., HALF]
    lower, packed = column_kinds()
    real_end = jnp.where(lower, real_0, real_32)
    real_end = jnp.where(packed, 0.5 * (real_0 - imag_32), real_end)
    imag_end = jnp.where(lower, imag_0, imag_32)
    imag_end = jnp.where(packed, 0.5 * (imag_0 + real_32), imag_end)
    first = jnp.arange(HALF) == 0
    real_half = jnp.where(first, real_end[..., None], real[..., :HALF])
    imag_half = jnp.where(first, imag_end[..., None], imag[..., :HALF])
    both = jnp.stack([real_half, imag_half], axis=1)
    return both.reshape(refs, 128, 128)


def energy_weights(spectral_weight):
    near, far = to_near(spectral_weight), to_far(spectral_weight)
    partner = jnp.where(jnp.arange(4 * BOX) < BOX, near, far)
    order, depth = np.zeros((KY_DEV, BOX, KY_DEV, BOX), np.float32), np.zeros((BOX, BOX), np.float32)
    for k in range(BOX):
        depth[k, -k % BOX] = 1.0
        for kyl in range(KY_DEV):
            order[kyl, -k % BOX, -kyl % KY_DEV, k] = 1.0
    highest = lax.Precision.HIGHEST
    other = jnp.dot(jnp.asarray(depth), partner, precision=highest)
    other = jnp.dot(other, jnp.asarray(order.reshape(256, 256)), precision=highest)
    fold = (spectral_weight + other).reshape(BOX, KY_DEV, BOX)
    fold_0, fold_32 = fold[..., 0], fold[..., HALF]
    lower, packed = column_kinds()
    end = jnp.where(packed, 0.25 * (fold_0 + fold_32), jnp.where(lower, fold_0, fold_32))
    cross = jnp.where(packed, 0.25 * (fold_0 - fold_32), 0.0)
    first = jnp.arange(HALF) == 0
    squares = jnp.where(first, end[..., None], fold[..., :HALF]).reshape(BOX, 128)
    products = jnp.where(first, cross[..., None], 0.0).reshape(BOX, 128)
    return jnp.tile(jnp.stack([squares, products]), (1, 2, 1))


def body(particles, counts, block_of, ref_index, references, spectral_weight):
    tomograms = lax.axis_size("tomo")
    rows = particles.shape[0]
    slots = 2 * tomograms
    refs = references.shape[0]
    positions = jnp.arange(rows, dtype=jnp.int32)

    is_live = positions < counts[0]
    same = (block_of[:, None] == block_of[None, :]) & is_live[:, None]
    before = positions[:, None] < positions[None, :]
    rank = jnp.sum((same & before).astype(jnp.int32), axis=0)
    slot_of = jnp.where(is_live, 2 * block_of + rank, slots)

    weights = energy_weights(spectral_weight)
    planes = half_planes(particles)
    pencils = lax.all_to_all(planes, "ref", split_axis=0, concat_axis=0, tiled=True)
    outgoing = half_spectra(slot_of, ref_index, pencils, weights, slots)
    arrived = lax.all_to_all(outgoing, "tomo", split_axis=0, concat_axis=0, tiled=True)
    coefficients = folded_references(references, spectral_weight)

    numbers = arrived.reshape(tomograms, 17, 2, 8, 128)[:, 16, :, 3, 0].reshape(slots)
    slot_index = numbers.astype(jnp.int32) - 1
    filled = slot_index >= 0
    slot_index = jnp.maximum(slot_index, 0)
    partial = jnp.sum(match(slot_index, arrived, coefficients), axis=2)
    spread = jnp.broadcast_to(partial.reshape(1, 1, 2 * slots), (16, 1, 2 * slots))
    gathered = lax.all_to_all(spread, "ref", split_axis=0, concat_axis=0, tiled=True)
    totals = jnp.sum(gathered, axis=(0, 1)).reshape(2, slots)
    particle_norm = jnp.sqrt(totals[1] / float(BOX) ** 3 + 1e-05)
    slot_scores = jnp.where(filled, totals[0] / (float(BOX) ** 1.5 * particle_norm), 0.0)
    gain = jnp.where(filled, jax.nn.sigmoid(slot_scores) / particle_norm, 0.0)
    gain = gain.astype(bf16).astype(f32)

    returned = lax.all_to_all(
        slot_scores.reshape(tomograms, 1, 2), "tomo", split_axis=0, concat_axis=0, tiled=True
    )
    half, half_sent = insert(slot_index, gain, arrived, refs)
    reconstruction = unfold(half, to_near(half_sent), to_far(half_sent))

    slot_match = slot_of[None, :] == jnp.arange(slots, dtype=jnp.int32)[:, None]
    row_scores = jnp.sum(jnp.where(slot_match, returned.reshape(slots)[:, None], 0.0), axis=0)
    return (row_scores, reconstruction)


def solution(mesh):
    placed = (
        P("tomo", "ref", None),
        P("tomo"),
        P("tomo"),
        P("tomo"),
        P("tomo", None, None, "ref"),
        P(None, "ref"),
    )
    return jax.shard_map(
        body,
        mesh=mesh,
        in_specs=placed,
        out_specs=(P("tomo"), P("tomo", None, None, "ref")),
        check_vma=False,
    )
```

```python
import numpy as np

import jax
import jax.numpy as jnp
import ml_dtypes
from jax import lax
from jax.experimental import pallas as pl
from jax.experimental.pallas import tpu as pltpu
from jax.sharding import PartitionSpec as P

BOX = 64
HALF = 32
KY_DEV = 4
f32 = jnp.float32
bf16 = jnp.bfloat16


def split_hi_lo(table):
    high = table.astype(np.float32).astype(ml_dtypes.bfloat16)
    low = (table - high.astype(np.float64)).astype(np.float32).astype(ml_dtypes.bfloat16)
    return high, low


def angles(a, b):
    return 2.0 * np.pi / BOX * (np.outer(a, b) % BOX)


def x_table():
    x = np.arange(BOX)
    phase = angles(x, np.arange(HALF))
    real, imag = np.cos(phase), -np.sin(phase)
    imag[:, 0] = np.cos(np.pi * x)
    one = np.concatenate([real, imag, imag, -real], axis=1)
    table = np.zeros((2, BOX, 2, 4 * HALF))
    table[0, :, 0], table[1, :, 1] = one, one
    return np.concatenate(split_hi_lo(table.reshape(2 * BOX, 8 * HALF)), axis=0)


def y_table():
    rows = np.arange(BOX)
    ky = KY_DEV * (rows % 16) + rows // 16
    y = np.concatenate([np.arange(0, BOX, 2), np.arange(1, BOX, 2)])
    cosine, sine = np.cos(angles(ky, y)), np.sin(angles(ky, y))
    zero = np.zeros_like(cosine)
    plain = np.concatenate([cosine, sine], axis=1)
    lower = ky[:, None] < 32
    packed = ky[:, None] % 32 == 0
    real = np.where(lower, np.concatenate([cosine, zero], 1), np.concatenate([zero, cosine], 1))
    imag = np.where(lower, np.concatenate([zero, sine], 1), np.concatenate([-sine, zero], 1))
    real, imag = np.where(packed, plain, real), np.where(packed, plain, imag)
    high, low = split_hi_lo(np.concatenate([plain, real, imag], axis=0))
    return np.concatenate(
        [
            np.concatenate([high, high], axis=1),
            np.concatenate([low, np.zeros_like(low)], axis=1),
        ],
        axis=0,
    )


def z_table():
    phase = angles(np.arange(BOX), np.arange(BOX))
    table = np.zeros((2, BOX, BOX, 2))
    table[0, :, :, 0], table[0, :, :, 1] = np.cos(phase), np.sin(phase)
    table[1, :, :, 0], table[1, :, :, 1] = -np.sin(phase), np.cos(phase)
    return np.concatenate(split_hi_lo(table.reshape(2 * BOX, 2 * BOX)), axis=1)


def reverse_table():
    reverse = np.zeros((2, BOX, 2, BOX))
    for kz in range(BOX):
        reverse[0, kz, 0, -kz % BOX], reverse[1, kz, 1, -kz % BOX] = 1.0, -1.0
    return reverse.reshape(2 * BOX, 2 * BOX).astype(ml_dtypes.bfloat16)


def unfold_table(j):
    own, mirror = np.zeros((KY_DEV, HALF, KY_DEV, BOX)), np.zeros((KY_DEV, HALF, KY_DEV, BOX))
    own_turned, mirror_turned = np.zeros_like(own), np.zeros_like(own)
    here, there = (0, HALF) if j < 8 else (HALF, 0)
    for kyl in range(KY_DEV):
        to = (KY_DEV - kyl) % KY_DEV
        if kyl == 0 and j % 8 == 0:
            own[0, 0, 0, 0] = mirror[0, 0, 0, 0] = 0.5
            own_turned[0, 0, 0, HALF], mirror_turned[0, 0, 0, HALF] = 0.5, -0.5
        else:
            own[kyl, 0, kyl, here] = mirror[kyl, 0, to, there] = 1.0
        for kx in range(1, HALF):
            own[kyl, kx, kyl, kx] = mirror[kyl, kx, to, BOX - kx] = 1.0
    stacked = np.concatenate([own, own, mirror, own_turned, own_turned, mirror_turned], axis=0)
    return stacked.reshape(6 * 2 * BOX, 4 * BOX).astype(ml_dtypes.bfloat16)


def table_of_device():
    j = lax.axis_index("ref")
    kind = jnp.where(j % 8 == 0, 2, 0) + jnp.where(j < 8, 0, 1)
    kinds = jnp.asarray(np.stack([unfold_table(k) for k in (1, 9, 0, 8)]))
    return lax.dynamic_index_in_dim(kinds, kind, keepdims=False)


def params(mebibytes=40):
    return pltpu.CompilerParams(vmem_limit_bytes=mebibytes * 2**20)


def cost(microseconds):
    return pl.CostEstimate(
        flops=0, bytes_accessed=int(microseconds * 3.0e6), transcendentals=0
    )


def dot(a, b):
    return jnp.dot(a, b, preferred_element_type=f32)


def planes_kernel(x_ref, table_ref, out_ref, rows_buf, turn_buf):
    lane = lax.broadcasted_iota(jnp.int32, (1, 128), 1)
    low_half = lane < 64
    even = lane % 64 < 32
    wide_lane = lax.broadcasted_iota(jnp.int32, (1, 256), 1) % 64
    for pair in range(x_ref.shape[0] // 2):
        for e in range(2):
            row = 2 * pair + e
            volume = x_ref[row].astype(f32)
            for yt in range(32):
                rows_buf[256 * row + 8 * yt : 256 * row + 8 * yt + 4, :] = volume[:, yt * 128 : (yt + 1) * 128]
            x = jnp.concatenate(
                [rows_buf[pl.ds(256 * row + zl, 32, stride=8), :] for zl in range(4)], axis=0
            ).astype(bf16)
            along = dot(jnp.concatenate([x, x], axis=1), table_ref[:256])
            tiles = []
            for zp in range(2):
                first, second = [], []
                for h in range(2):
                    a = along[64 * zp : 64 * zp + 32, 128 * h : 128 * h + 128]
                    b = along[64 * zp + 32 : 64 * zp + 64, 128 * h : 128 * h + 128]
                    first.append(jnp.where(low_half, a, pltpu.roll(b, 64, 1)))
                    second.append(jnp.where(low_half, pltpu.roll(a, 64, 1), b))
                tiles.append(jnp.concatenate(first + second, axis=0))
            wide = jnp.concatenate(tiles, axis=1)
            high = wide.astype(bf16)
            low = (wide - high.astype(f32)).astype(bf16)
            full = dot(table_ref[256:], jnp.concatenate([high, low], axis=0))
            full = full[:192] + full[192:]
            planes = jnp.where(wide_lane == 0, full[64:128], full[:64])
            planes = jnp.where(wide_lane == 32, full[128:], planes)
            for zp in range(2):
                i0, i1, i2, i3 = (
                    planes[16 * k : 16 * k + 16, 128 * zp : 128 * zp + 128] for k in range(4)
                )
                p0 = jnp.where(low_half, i0, pltpu.roll(i2, 64, 1))
                p2 = jnp.where(low_half, pltpu.roll(i0, 64, 1), i2)
                p1 = jnp.where(low_half, i1, pltpu.roll(i3, 64, 1))
                p3 = jnp.where(low_half, pltpu.roll(i1, 64, 1), i3)
                turned = (
                    jnp.where(even, p0, pltpu.roll(p1, 32, 1)),
                    jnp.where(even, pltpu.roll(p0, 96, 1), p1),
                    jnp.where(even, p2, pltpu.roll(p3, 32, 1)),
                    jnp.where(even, pltpu.roll(p2, 96, 1), p3),
                )
                for g in range(4):
                    start = 128 * row + (4 * zp + g) * 16
                    turn_buf[start : start + 16, :] = turned[g]
        for j in range(16):
            both = [turn_buf[pl.ds(128 * (2 * pair + e) + j, 8, stride=16), :] for e in range(2)]
            out_ref[j, pair] = jnp.concatenate(both, axis=0).astype(bf16)


def half_planes(particles):
    rows = particles.shape[0]
    group = 4
    return pl.pallas_call(
        planes_kernel,
        grid=(rows // group,),
        in_specs=[
            pl.BlockSpec((group, 4, BOX * BOX), lambda i: (i, 0, 0)),
            pl.BlockSpec((640, 256), lambda i: (0, 0)),
        ],
        out_specs=pl.BlockSpec((16, group // 2, 16, 128), lambda i: (0, i, 0, 0)),
        out_shape=jax.ShapeDtypeStruct((16, rows // 2, 16, 128), bf16),
        scratch_shapes=[
            pltpu.VMEM((group * 256, 128), f32),
            pltpu.VMEM((group * 128, 128), f32),
        ],
        compiler_params=params(58),
        cost_estimate=cost(8.0),
        name="half_planes",
    )(particles, jnp.asarray(np.concatenate([x_table(), y_table()], axis=0)))


def depth_kernel(slot_ref, index_ref, b_ref, table_ref, weight_ref, send_ref, extra_buf):
    slots = extra_buf.shape[0]
    tomograms = slots // 2
    together = 4
    line = lax.broadcasted_iota(jnp.int32, (8, 128), 0)
    extra_buf[...] = jnp.zeros_like(extra_buf)

    def step(i, _):
        done = []
        for p in range(together):
            block = b_ref[:, together * i + p].astype(f32)
            a = block[:, :8, :].reshape(128, 128)
            b = block[:, 8:, :].reshape(128, 128)
            pencils = jnp.concatenate([a, b], axis=1).astype(bf16)
            spectra = dot(table_ref[:128], jnp.concatenate([pencils, pencils], axis=0)).astype(bf16)
            turned = dot(table_ref[128:, :128], spectra)
            for e in range(2):
                one = spectra[:, 128 * e : 128 * e + 128]
                terms = turned[:, 128 * e : 128 * e + 128] * weight_ref[...]
                cross = jnp.sum(one.astype(f32) * terms, axis=0, keepdims=True)
                high = cross.astype(bf16).astype(f32)
                middle = (cross - high).astype(bf16).astype(f32)
                low = cross - high - middle
                number = (index_ref[2 * (together * i + p) + e] + 1).astype(f32)
                extra = jnp.where(line == 0, high, jnp.where(line == 1, middle, low))
                done.append((one, jnp.where(line == 3, number, extra)))
        for r in range(2 * together):
            one, extra = done[r]
            slot = slot_ref[2 * together * i + r]

            @pl.when(slot < slots)
            def _():
                send_ref[pl.ds(17 * (slot // 2) + 8 * (slot % 2), 8)] = one.reshape(8, 16, 128)
                extra_buf[slot] = extra

        return 0

    lax.fori_loop(0, b_ref.shape[1] // together, step, 0)

    for t in range(tomograms):
        both = jnp.concatenate([extra_buf[2 * t], extra_buf[2 * t + 1]], axis=0)
        send_ref[17 * t + 16] = both.astype(bf16)


def half_spectra(slot_of, ref_index, pencils, weights, slots):
    vmem = pl.BlockSpec(memory_space=pltpu.VMEM)
    smem = pl.BlockSpec(memory_space=pltpu.SMEM)
    reverse = np.concatenate([reverse_table(), np.zeros_like(reverse_table())], axis=1)
    return pl.pallas_call(
        depth_kernel,
        in_specs=[smem, smem, vmem, vmem, vmem],
        out_specs=vmem,
        out_shape=jax.ShapeDtypeStruct((slots // 2 * 17, 16, 128), bf16),
        scratch_shapes=[pltpu.VMEM((slots, 8, 128), f32)],
        compiler_params=params(),
        cost_estimate=cost(4.0),
        name="half_spectra",
    )(slot_of, ref_index, pencils, jnp.asarray(np.concatenate([z_table(), reverse])), weights)


def match_kernel(index_ref, spec_ref, coef_ref, weight_ref, out_ref):
    group = spec_ref.shape[0] // 17
    base = pl.program_id(0) * 2 * group
    for t in range(group):
        extra = spec_ref[17 * t + 16].astype(f32)
        for k in range(2):
            s = 2 * t + k
            value = spec_ref[17 * t + 8 * k : 17 * t + 8 * k + 8].reshape(128, 128).astype(f32)
            product = value * coef_ref[index_ref[base + s]]
            out_ref[0, s : s + 1, :] = jnp.sum(product, axis=0, keepdims=True)
            squares = jnp.sum(value * value * weight_ref[...], axis=0, keepdims=True)
            parts = jnp.sum(extra[8 * k : 8 * k + 3], axis=0, keepdims=True)
            out_ref[1, s : s + 1, :] = squares + parts


def match(index, arrived, coefficients, weights):
    slots = index.shape[0]
    refs = coefficients.shape[0]
    group = min(4, slots // 2)
    return pl.pallas_call(
        match_kernel,
        grid_spec=pltpu.PrefetchScalarGridSpec(
            num_scalar_prefetch=1,
            grid=(slots // 2 // group,),
            in_specs=[
                pl.BlockSpec((17 * group, 16, 128), lambda i, _: (i, 0, 0)),
                pl.BlockSpec((refs, 128, 128), lambda i, _: (0, 0, 0)),
                pl.BlockSpec((128, 128), lambda i, _: (0, 0)),
            ],
            out_specs=pl.BlockSpec((2, 2 * group, 128), lambda i, _: (0, i, 0)),
        ),
        out_shape=jax.ShapeDtypeStruct((2, slots, 128), f32),
        compiler_params=params(),
        cost_estimate=cost(2.0),
        name="match",
    )(index, arrived, coefficients, weights)


def insert_kernel(index_ref, gain_ref, spec_ref, out_ref, sent_ref):
    group = spec_ref.shape[0] // 17
    step = pl.program_id(0)

    @pl.when(step == 0)
    def _():
        out_ref[...] = jnp.zeros_like(out_ref)

    for t in range(group):
        for k in range(2):
            slot = step * 2 * group + 2 * t + k
            value = spec_ref[17 * t + 8 * k : 17 * t + 8 * k + 8].reshape(128, 128).astype(f32)
            gain = gain_ref[slot]
            out_ref[index_ref[slot]] += jnp.where(gain > 0.0, gain * value, 0.0)

    @pl.when(step == pl.num_programs(0) - 1)
    def _():
        sent_ref[...] = out_ref[...].astype(bf16)


def insert(index, gain, arrived, refs):
    slots = index.shape[0]
    group = min(4, slots // 2)
    whole = pl.BlockSpec((refs, 128, 128), lambda i, *_: (0, 0, 0))
    return pl.pallas_call(
        insert_kernel,
        grid_spec=pltpu.PrefetchScalarGridSpec(
            num_scalar_prefetch=2,
            grid=(slots // 2 // group,),
            in_specs=[pl.BlockSpec((17 * group, 16, 128), lambda i, *_: (i, 0, 0))],
            out_specs=[whole, whole],
        ),
        out_shape=[
            jax.ShapeDtypeStruct((refs, 128, 128), f32),
            jax.ShapeDtypeStruct((refs, 128, 128), bf16),
        ],
        compiler_params=params(),
        cost_estimate=cost(25.0),
        name="insert",
    )(index, gain, arrived)


def unfold_kernel(own_ref, near_ref, far_ref, q_ref, reverse_ref, out_ref):
    lane = lax.broadcasted_iota(jnp.int32, (1, 128), 1)
    own = own_ref[...]
    partner = jnp.where(lane < HALF, near_ref[...].astype(f32), far_ref[...].astype(f32)).astype(bf16)
    conjugate = dot(reverse_ref[...], partner)

    def turned(v):
        return jnp.concatenate([v[64:], -v[:64]], axis=0)

    high = own.astype(bf16).astype(f32)
    parts = [high, own - high, conjugate]
    parts = parts + [turned(v) for v in parts]
    full = dot(jnp.concatenate(parts, axis=1).astype(bf16), q_ref[...])
    for lt in range(2):
        for c in range(2):
            out_ref[pl.ds(2 * lt + c, 64, stride=4), :] = full[
                64 * c : 64 * c + 64, 128 * lt : 128 * lt + 128
            ]


def unfold(own, near, far, table):
    refs = own.shape[0]
    one = pl.BlockSpec((None, 128, 128), lambda i: (i, 0, 0))
    packed = pl.pallas_call(
        unfold_kernel,
        grid=(refs,),
        in_specs=[
            one,
            one,
            one,
            pl.BlockSpec((768, 256), lambda i: (0, 0)),
            pl.BlockSpec((128, 128), lambda i: (0, 0)),
        ],
        out_specs=pl.BlockSpec((None, 256, 128), lambda i: (i, 0, 0)),
        out_shape=jax.ShapeDtypeStruct((refs, 256, 128), f32),
        compiler_params=params(),
        cost_estimate=cost(0.5),
        name="unfold",
    )(own, near, far, table, jnp.asarray(reverse_table()))
    tiles = packed.reshape(refs, BOX, 2, 2, 128)
    return tiles.transpose(0, 1, 3, 2, 4).reshape(refs, BOX, 2, 256)


def to_far(values):
    return lax.ppermute(values, "ref", [(j, 15 - j) for j in range(16)])


def to_near(values):
    return lax.ppermute(values, "ref", [(j, -j % 16) for j in range(16)])


def mirrored(values, ky_axis):
    near = to_near(lax.slice_in_dim(values, 0, 1, axis=ky_axis))
    far = to_far(lax.slice_in_dim(values, 1, KY_DEV, axis=ky_axis))
    return jnp.concatenate([near, lax.rev(far, (ky_axis,))], axis=ky_axis)


def minus_index(values, axis):
    return jnp.roll(lax.rev(values, (axis,)), 1, axis)


def minus_kx(values):
    order = np.zeros((BOX, BOX), np.float32)
    for kx in range(BOX):
        order[-kx % BOX, kx] = 1.0
    return jnp.einsum(
        "...x,xk->...k", values, jnp.asarray(order, values.dtype), precision=lax.Precision.HIGHEST,
        preferred_element_type=f32,
    )


def column_kinds():
    j = lax.axis_index("ref")
    return j < 8, (j % 8 == 0) & (jnp.arange(KY_DEV) == 0)


def folded_references(references, spectral_weight):
    refs = references.shape[0]
    weighted = (spectral_weight[None, :, None, :] * references.astype(f32)).astype(bf16)
    weighted = weighted.reshape(refs, BOX, 2, KY_DEV, BOX)
    other = minus_kx(minus_index(mirrored(weighted, 3), 1))
    weighted = weighted.astype(f32)
    real = weighted[:, :, 0] + other[:, :, 0]
    imag = weighted[:, :, 1] - other[:, :, 1]
    real_0, real_32 = real[..., 0], real[..., HALF]
    imag_0, imag_32 = imag[..., 0], imag[..., HALF]
    lower, packed = column_kinds()
    real_end = jnp.where(lower, real_0, real_32)
    real_end = jnp.where(packed, 0.5 * (real_0 - imag_32), real_end)
    imag_end = jnp.where(lower, imag_0, imag_32)
    imag_end = jnp.where(packed, 0.5 * (imag_0 + real_32), imag_end)
    first = jnp.arange(HALF) == 0
    real_half = jnp.where(first, real_end[..., None], real[..., :HALF])
    imag_half = jnp.where(first, imag_end[..., None], imag[..., :HALF])
    both = jnp.stack([real_half, imag_half], axis=1)
    return both.reshape(refs, 128, 128)


def product_weights(spectral_weight):
    ends = spectral_weight[:, : HALF + 1 : HALF]
    ends = ends + minus_index(ends, 0)
    _, packed = column_kinds()
    cross = jnp.where(packed[0], 0.25 * (ends[:, :1] - ends[:, 1:]), 0.0)
    return jnp.tile(jnp.where(jnp.arange(128) == 0, cross, 0.0), (2, 1))


def square_weights(spectral_weight):
    near, far = to_near(spectral_weight), to_far(spectral_weight)
    partner = jnp.where(jnp.arange(4 * BOX) < BOX, near, far)
    order, depth = np.zeros((KY_DEV, BOX, KY_DEV, BOX), np.float32), np.zeros((BOX, BOX), np.float32)
    for k in range(BOX):
        depth[k, -k % BOX] = 1.0
        for kyl in range(KY_DEV):
            order[kyl, -k % BOX, -kyl % KY_DEV, k] = 1.0
    highest = lax.Precision.HIGHEST
    other = jnp.dot(jnp.asarray(depth), partner, precision=highest)
    other = jnp.dot(other, jnp.asarray(order.reshape(256, 256)), precision=highest)
    fold = (spectral_weight + other).reshape(BOX, KY_DEV, BOX)
    fold_0, fold_32 = fold[..., 0], fold[..., HALF]
    lower, packed = column_kinds()
    end = jnp.where(packed, 0.25 * (fold_0 + fold_32), jnp.where(lower, fold_0, fold_32))
    first = jnp.arange(HALF) == 0
    squares = jnp.where(first, end[..., None], fold[..., :HALF]).reshape(BOX, 128)
    return jnp.tile(squares, (2, 1))


def body(particles, counts, block_of, ref_index, references, spectral_weight):
    tomograms = lax.axis_size("tomo")
    rows = particles.shape[0]
    slots = 2 * tomograms
    refs = references.shape[0]
    positions = jnp.arange(rows, dtype=jnp.int32)

    is_live = positions < counts[0]
    same = (block_of[:, None] == block_of[None, :]) & is_live[:, None]
    before = positions[:, None] < positions[None, :]
    rank = jnp.sum((same & before).astype(jnp.int32), axis=0)
    slot_of = jnp.where(is_live, 2 * block_of + rank, slots)

    planes = half_planes(particles)
    pencils = lax.all_to_all(planes, "ref", split_axis=0, concat_axis=0, tiled=True)
    outgoing = half_spectra(
        slot_of, ref_index, pencils, product_weights(spectral_weight), slots
    )
    arrived = lax.all_to_all(outgoing, "tomo", split_axis=0, concat_axis=0, tiled=True)
    coefficients, table = lax.optimization_barrier(
        (folded_references(references, spectral_weight), table_of_device())
    )

    numbers = arrived.reshape(tomograms, 17, 2, 8, 128)[:, 16, :, 3, 0].reshape(slots)
    slot_index = numbers.astype(jnp.int32) - 1
    filled = slot_index >= 0
    slot_index = jnp.maximum(slot_index, 0)
    partial = jnp.sum(match(slot_index, arrived, coefficients, square_weights(spectral_weight)), axis=2)
    spread = jnp.broadcast_to(partial.reshape(1, 1, 2 * slots), (16, 1, 2 * slots))
    gathered = lax.all_to_all(spread, "ref", split_axis=0, concat_axis=0, tiled=True)
    totals = jnp.sum(gathered, axis=(0, 1)).reshape(2, slots)
    particle_norm = jnp.sqrt(totals[1] / float(BOX) ** 3 + 1e-05)
    slot_scores = jnp.where(filled, totals[0] / (float(BOX) ** 1.5 * particle_norm), 0.0)
    gain = jnp.where(filled, jax.nn.sigmoid(slot_scores) / particle_norm, 0.0)
    gain = gain.astype(bf16).astype(f32)

    returned = lax.all_to_all(
        slot_scores.reshape(tomograms, 1, 2), "tomo", split_axis=0, concat_axis=0, tiled=True
    )
    half, half_sent = insert(slot_index, gain, arrived, refs)
    reconstruction = unfold(half, to_near(half_sent), to_far(half_sent), table)
    returned, reconstruction = lax.optimization_barrier((returned, reconstruction))

    slot_ids = jnp.arange(slots, dtype=jnp.int32).reshape(tomograms, 1, 2, 1)
    row_scores = jnp.sum(jnp.where(slot_of == slot_ids, returned[..., None], 0.0), axis=(0, 1, 2))
    return (row_scores, reconstruction)


def solution(mesh):
    placed = (
        P("tomo", "ref", None),
        P("tomo"),
        P("tomo"),
        P("tomo"),
        P("tomo", None, None, "ref"),
        P(None, "ref"),
    )
    return jax.shard_map(
        body,
        mesh=mesh,
        in_specs=placed,
        out_specs=(P("tomo"), P("tomo", None, None, "ref")),
        check_vma=False,
    )
```

```python
import numpy as np

import jax
import jax.numpy as jnp
import ml_dtypes
from jax import lax
from jax.experimental import pallas as pl
from jax.experimental.pallas import tpu as pltpu
from jax.sharding import PartitionSpec as P

BOX = 64
HALF = 32
KY_DEV = 4
f32 = jnp.float32
bf16 = jnp.bfloat16


def split_hi_lo(table):
    high = table.astype(np.float32).astype(ml_dtypes.bfloat16)
    low = (table - high.astype(np.float64)).astype(np.float32).astype(ml_dtypes.bfloat16)
    return high, low


def angles(a, b):
    return 2.0 * np.pi / BOX * (np.outer(a, b) % BOX)


def x_table():
    x = np.arange(BOX)
    phase = angles(x, np.arange(HALF))
    real, imag = np.cos(phase), -np.sin(phase)
    imag[:, 0] = np.cos(np.pi * x)
    one = np.concatenate([real, imag, imag, -real], axis=1)
    table = np.zeros((2, BOX, 2, 4 * HALF))
    table[0, :, 0], table[1, :, 1] = one, one
    return np.concatenate(split_hi_lo(table.reshape(2 * BOX, 8 * HALF)), axis=0)


def y_table():
    rows = np.arange(BOX)
    ky = KY_DEV * (rows % 16) + rows // 16
    y = np.concatenate([np.arange(0, BOX, 2), np.arange(1, BOX, 2)])
    cosine, sine = np.cos(angles(ky, y)), np.sin(angles(ky, y))
    zero = np.zeros_like(cosine)
    plain = np.concatenate([cosine, sine], axis=1)
    lower = ky[:, None] < 32
    packed = ky[:, None] % 32 == 0
    real = np.where(lower, np.concatenate([cosine, zero], 1), np.concatenate([zero, cosine], 1))
    imag = np.where(lower, np.concatenate([zero, sine], 1), np.concatenate([-sine, zero], 1))
    real, imag = np.where(packed, plain, real), np.where(packed, plain, imag)
    high, low = split_hi_lo(np.concatenate([plain, real, imag], axis=0))
    return np.concatenate(
        [
            np.concatenate([high, high], axis=1),
            np.concatenate([low, np.zeros_like(low)], axis=1),
        ],
        axis=0,
    )


def z_table():
    phase = angles(np.arange(BOX), np.arange(BOX))
    table = np.zeros((2, BOX, BOX, 2))
    table[0, :, :, 0], table[0, :, :, 1] = np.cos(phase), np.sin(phase)
    table[1, :, :, 0], table[1, :, :, 1] = -np.sin(phase), np.cos(phase)
    return np.concatenate(split_hi_lo(table.reshape(2 * BOX, 2 * BOX)), axis=1)


def reverse_table():
    reverse = np.zeros((2, BOX, 2, BOX))
    for kz in range(BOX):
        reverse[0, kz, 0, -kz % BOX], reverse[1, kz, 1, -kz % BOX] = 1.0, -1.0
    return reverse.reshape(2 * BOX, 2 * BOX).astype(ml_dtypes.bfloat16)


def unfold_table(j):
    own, mirror = np.zeros((KY_DEV, HALF, KY_DEV, BOX)), np.zeros((KY_DEV, HALF, KY_DEV, BOX))
    own_turned, mirror_turned = np.zeros_like(own), np.zeros_like(own)
    here, there = (0, HALF) if j < 8 else (HALF, 0)
    for kyl in range(KY_DEV):
        to = (KY_DEV - kyl) % KY_DEV
        if kyl == 0 and j % 8 == 0:
            own[0, 0, 0, 0] = mirror[0, 0, 0, 0] = 0.5
            own_turned[0, 0, 0, HALF], mirror_turned[0, 0, 0, HALF] = 0.5, -0.5
        else:
            own[kyl, 0, kyl, here] = mirror[kyl, 0, to, there] = 1.0
        for kx in range(1, HALF):
            own[kyl, kx, kyl, kx] = mirror[kyl, kx, to, BOX - kx] = 1.0
    stacked = np.concatenate([own, own, mirror, own_turned, own_turned, mirror_turned], axis=0)
    return stacked.reshape(6 * 2 * BOX, 4 * BOX).astype(ml_dtypes.bfloat16)


def table_of_device():
    j = lax.axis_index("ref")
    kind = jnp.where(j % 8 == 0, 2, 0) + jnp.where(j < 8, 0, 1)
    kinds = jnp.asarray(np.stack([unfold_table(k) for k in (1, 9, 0, 8)]))
    return lax.dynamic_index_in_dim(kinds, kind, keepdims=False)


def params(mebibytes=40):
    return pltpu.CompilerParams(vmem_limit_bytes=mebibytes * 2**20)


def cost(microseconds):
    return pl.CostEstimate(
        flops=0, bytes_accessed=int(microseconds * 3.0e6), transcendentals=0
    )


def dot(a, b):
    return jnp.dot(a, b, preferred_element_type=f32)


def planes_kernel(x_ref, table_ref, out_ref, rows_buf, turn_buf):
    lane = lax.broadcasted_iota(jnp.int32, (1, 128), 1)
    low_half = lane < 64
    even = lane % 64 < 32
    wide_lane = lax.broadcasted_iota(jnp.int32, (1, 256), 1) % 64
    group = x_ref.shape[0]
    for row in range(group):
        volume = x_ref[row].astype(f32)
        for yt in range(32):
            start = 256 * row + 8 * yt
            rows_buf[start : start + 4, :] = volume[:, yt * 128 : (yt + 1) * 128]
    x = jnp.concatenate(
        [
            rows_buf[pl.ds(256 * row + zl, 32, stride=8), :]
            for row in range(group)
            for zl in range(4)
        ],
        axis=0,
    ).astype(bf16)
    along = dot(jnp.concatenate([x, x], axis=1), table_ref[:256])
    for row in range(group):
        tiles = []
        for zp in range(2):
            first, second = [], []
            start = 128 * row + 64 * zp
            for h in range(2):
                a = along[start : start + 32, 128 * h : 128 * h + 128]
                b = along[start + 32 : start + 64, 128 * h : 128 * h + 128]
                first.append(jnp.where(low_half, a, pltpu.roll(b, 64, 1)))
                second.append(jnp.where(low_half, pltpu.roll(a, 64, 1), b))
            tiles.append(jnp.concatenate(first + second, axis=0))
        wide = jnp.concatenate(tiles, axis=1)
        high = wide.astype(bf16)
        low = (wide - high.astype(f32)).astype(bf16)
        full = dot(table_ref[256:], jnp.concatenate([high, low], axis=0))
        full = full[:192] + full[192:]
        planes = jnp.where(wide_lane == 0, full[64:128], full[:64])
        planes = jnp.where(wide_lane == 32, full[128:], planes)
        for zp in range(2):
            i0, i1, i2, i3 = (
                planes[16 * k : 16 * k + 16, 128 * zp : 128 * zp + 128] for k in range(4)
            )
            p0 = jnp.where(low_half, i0, pltpu.roll(i2, 64, 1))
            p2 = jnp.where(low_half, pltpu.roll(i0, 64, 1), i2)
            p1 = jnp.where(low_half, i1, pltpu.roll(i3, 64, 1))
            p3 = jnp.where(low_half, pltpu.roll(i1, 64, 1), i3)
            turned = (
                jnp.where(even, p0, pltpu.roll(p1, 32, 1)),
                jnp.where(even, pltpu.roll(p0, 96, 1), p1),
                jnp.where(even, p2, pltpu.roll(p3, 32, 1)),
                jnp.where(even, pltpu.roll(p2, 96, 1), p3),
            )
            for g in range(4):
                start = 128 * row + (4 * zp + g) * 16
                turn_buf[start : start + 16, :] = turned[g]
    for pair in range(group // 2):
        for j in range(16):
            both = [turn_buf[pl.ds(128 * (2 * pair + e) + j, 8, stride=16), :] for e in range(2)]
            out_ref[j, pair] = jnp.concatenate(both, axis=0).astype(bf16)


def half_planes(particles):
    rows = particles.shape[0]
    group = 16
    return pl.pallas_call(
        planes_kernel,
        grid=(rows // group,),
        in_specs=[
            pl.BlockSpec((group, 4, BOX * BOX), lambda i: (i, 0, 0)),
            pl.BlockSpec((640, 256), lambda i: (0, 0)),
        ],
        out_specs=pl.BlockSpec((16, group // 2, 16, 128), lambda i: (0, i, 0, 0)),
        out_shape=jax.ShapeDtypeStruct((16, rows // 2, 16, 128), bf16),
        scratch_shapes=[
            pltpu.VMEM((group * 256, 128), f32),
            pltpu.VMEM((group * 128, 128), f32),
        ],
        compiler_params=params(58),
        cost_estimate=cost(8.0),
        name="half_planes",
    )(particles, jnp.asarray(np.concatenate([x_table(), y_table()], axis=0)))


def depth_kernel(slot_ref, index_ref, b_ref, table_ref, weight_ref, send_ref, *scratch):
    spec_buf, extra_buf, packed_buf, sems = scratch
    slots = extra_buf.shape[0]
    tomograms = slots // 2
    together = 4
    line = lax.broadcasted_iota(jnp.int32, (4, 128), 0)
    extra_buf[...] = jnp.zeros_like(extra_buf)

    def routed(row):
        slot = slot_ref[row]
        target = send_ref.at[slot // 2, pl.ds(16 * (slot % 2), 16)]
        return slot, pltpu.make_async_copy(spec_buf.at[row], target, sems.at[row])

    def step(i, _):
        for p in range(together):
            block = b_ref[:, together * i + p].astype(f32)
            a = block[:, :8, :].reshape(128, 128)
            b = block[:, 8:, :].reshape(128, 128)
            pencils = jnp.concatenate([a, b], axis=1).astype(bf16)
            exact = dot(table_ref[:128], jnp.concatenate([pencils, pencils], axis=0))
            spectra = exact.astype(bf16)
            turned = dot(table_ref[128:, :128], spectra)
            for e in range(2):
                row = 2 * (together * i + p) + e
                one = exact[:, 128 * e : 128 * e + 128]
                spec_buf[row] = one.reshape(16, 8, 128).astype(bf16)
                terms = turned[:, 128 * e : 128 * e + 128] * weight_ref[...]
                value = spectra[:, 128 * e : 128 * e + 128].astype(f32)
                cross = jnp.sum(value * terms, axis=0, keepdims=True)
                high = cross.astype(bf16).astype(f32)
                middle = (cross - high).astype(bf16).astype(f32)
                low = cross - high - middle
                number = (index_ref[row] + 1).astype(f32)
                extra = jnp.where(line == 0, high, jnp.where(line == 1, middle, low))
                extra = jnp.where(line == 3, number, extra)
                slot = slot_ref[row]

                @pl.when(slot < slots)
                def _():
                    extra_buf[slot] = extra

        for r in range(2 * together):
            slot, copy = routed(2 * together * i + r)

            @pl.when(slot < slots)
            def _():
                copy.start()

        return 0

    lax.fori_loop(0, b_ref.shape[1] // together, step, 0)

    for t in range(tomograms):
        both = jnp.concatenate([extra_buf[2 * t], extra_buf[2 * t + 1]], axis=0)
        packed_buf[t] = both.astype(bf16)
    last = pltpu.make_async_copy(packed_buf, send_ref.at[:, 32], sems.at[sems.shape[0] - 1])
    last.start()

    def finish(row, _):
        slot, copy = routed(row)

        @pl.when(slot < slots)
        def _():
            copy.wait()

        return 0

    lax.fori_loop(0, 2 * b_ref.shape[1], finish, 0)
    last.wait()


def half_spectra(slot_of, ref_index, pencils, weights, slots):
    vmem = pl.BlockSpec(memory_space=pltpu.VMEM)
    smem = pl.BlockSpec(memory_space=pltpu.SMEM)
    rows = 2 * pencils.shape[1]
    reverse = np.concatenate([reverse_table(), np.zeros_like(reverse_table())], axis=1)
    return pl.pallas_call(
        depth_kernel,
        in_specs=[smem, smem, vmem, vmem, vmem],
        out_specs=pl.BlockSpec(memory_space=pl.ANY),
        out_shape=jax.ShapeDtypeStruct((slots // 2, 33, 8, 128), bf16),
        scratch_shapes=[
            pltpu.VMEM((rows, 16, 8, 128), bf16),
            pltpu.VMEM((slots, 4, 128), f32),
            pltpu.VMEM((slots // 2, 8, 128), bf16),
            pltpu.SemaphoreType.DMA((rows + 1,)),
        ],
        compiler_params=params(58),
        cost_estimate=cost(4.0),
        name="half_spectra",
    )(slot_of, ref_index, pencils, jnp.asarray(np.concatenate([z_table(), reverse])), weights)


def match_kernel(index_ref, spec_ref, coef_ref, weight_ref, out_ref):
    group = spec_ref.shape[0]
    base = pl.program_id(0) * 2 * group
    for t in range(group):
        extra = spec_ref[t, 32].astype(f32)
        for k in range(2):
            s = 2 * t + k
            value = spec_ref[t, 16 * k : 16 * k + 16].astype(f32).reshape(128, 128)
            product = value * coef_ref[index_ref[base + s]]
            out_ref[0, s : s + 1, :] = jnp.sum(product, axis=0, keepdims=True)
            squares = jnp.sum(value * value * weight_ref[...], axis=0, keepdims=True)
            parts = jnp.sum(extra[4 * k : 4 * k + 3], axis=0, keepdims=True)
            out_ref[1, s : s + 1, :] = squares + parts


def match(index, arrived, coefficients, weights):
    slots = index.shape[0]
    refs = coefficients.shape[0]
    group = min(4, slots // 2)
    return pl.pallas_call(
        match_kernel,
        grid_spec=pltpu.PrefetchScalarGridSpec(
            num_scalar_prefetch=1,
            grid=(slots // 2 // group,),
            in_specs=[
                pl.BlockSpec((group, 33, 8, 128), lambda i, _: (i, 0, 0, 0)),
                pl.BlockSpec((refs, 128, 128), lambda i, _: (0, 0, 0)),
                pl.BlockSpec((128, 128), lambda i, _: (0, 0)),
            ],
            out_specs=pl.BlockSpec((2, 2 * group, 128), lambda i, _: (0, i, 0)),
        ),
        out_shape=jax.ShapeDtypeStruct((2, slots, 128), f32),
        compiler_params=params(),
        cost_estimate=cost(2.0),
        name="match",
    )(index, arrived, coefficients, weights)


def insert_kernel(index_ref, gain_ref, spec_ref, out_ref, sent_ref):
    group = spec_ref.shape[0]
    step = pl.program_id(0)

    @pl.when(step == 0)
    def _():
        out_ref[...] = jnp.zeros_like(out_ref)

    for t in range(group):
        for k in range(2):
            slot = step * 2 * group + 2 * t + k
            value = spec_ref[t, 16 * k : 16 * k + 16].astype(f32).reshape(128, 128)
            gain = gain_ref[slot]
            out_ref[index_ref[slot]] += jnp.where(gain > 0.0, gain * value, 0.0)

    @pl.when(step == pl.num_programs(0) - 1)
    def _():
        sent_ref[...] = out_ref[...].astype(bf16)


def insert(index, gain, arrived, refs):
    slots = index.shape[0]
    group = min(4, slots // 2)
    whole = pl.BlockSpec((refs, 128, 128), lambda i, *_: (0, 0, 0))
    return pl.pallas_call(
        insert_kernel,
        grid_spec=pltpu.PrefetchScalarGridSpec(
            num_scalar_prefetch=2,
            grid=(slots // 2 // group,),
            in_specs=[pl.BlockSpec((group, 33, 8, 128), lambda i, *_: (i, 0, 0, 0))],
            out_specs=[whole, whole],
        ),
        out_shape=[
            jax.ShapeDtypeStruct((refs, 128, 128), f32),
            jax.ShapeDtypeStruct((refs, 128, 128), bf16),
        ],
        compiler_params=params(),
        cost_estimate=cost(25.0),
        name="insert",
    )(index, gain, arrived)


def unfold_kernel(own_ref, near_ref, far_ref, q_ref, reverse_ref, out_ref):
    lane = lax.broadcasted_iota(jnp.int32, (1, 128), 1)
    own = own_ref[...]
    partner = jnp.where(lane < HALF, near_ref[...].astype(f32), far_ref[...].astype(f32)).astype(bf16)
    conjugate = dot(reverse_ref[...], partner)

    def turned(v):
        return jnp.concatenate([v[64:], -v[:64]], axis=0)

    high = own.astype(bf16).astype(f32)
    parts = [high, own - high, conjugate]
    parts = parts + [turned(v) for v in parts]
    full = dot(jnp.concatenate(parts, axis=1).astype(bf16), q_ref[...])
    for lt in range(2):
        for c in range(2):
            out_ref[pl.ds(2 * lt + c, 64, stride=4), :] = full[
                64 * c : 64 * c + 64, 128 * lt : 128 * lt + 128
            ]


def unfold(own, near, far, table):
    refs = own.shape[0]
    one = pl.BlockSpec((None, 128, 128), lambda i: (i, 0, 0))
    packed = pl.pallas_call(
        unfold_kernel,
        grid=(refs,),
        in_specs=[
            one,
            one,
            one,
            pl.BlockSpec((768, 256), lambda i: (0, 0)),
            pl.BlockSpec((128, 128), lambda i: (0, 0)),
        ],
        out_specs=pl.BlockSpec((None, 256, 128), lambda i: (i, 0, 0)),
        out_shape=jax.ShapeDtypeStruct((refs, 256, 128), f32),
        compiler_params=params(),
        cost_estimate=cost(0.5),
        name="unfold",
    )(own, near, far, table, jnp.asarray(reverse_table()))
    tiles = packed.reshape(refs, BOX, 2, 2, 128)
    return tiles.transpose(0, 1, 3, 2, 4).reshape(refs, BOX, 2, 256)


def to_far(values):
    return lax.ppermute(values, "ref", [(j, 15 - j) for j in range(16)])


def to_near(values):
    return lax.ppermute(values, "ref", [(j, -j % 16) for j in range(16)])


def mirrored(values, ky_axis):
    near = to_near(lax.slice_in_dim(values, 0, 1, axis=ky_axis))
    far = to_far(lax.slice_in_dim(values, 1, KY_DEV, axis=ky_axis))
    return jnp.concatenate([near, lax.rev(far, (ky_axis,))], axis=ky_axis)


def minus_index(values, axis):
    return jnp.roll(lax.rev(values, (axis,)), 1, axis)


def minus_kx(values):
    order = np.zeros((BOX, BOX), np.float32)
    for kx in range(BOX):
        order[-kx % BOX, kx] = 1.0
    return jnp.einsum(
        "...x,xk->...k", values, jnp.asarray(order, values.dtype), precision=lax.Precision.HIGHEST,
        preferred_element_type=f32,
    )


def column_kinds():
    j = lax.axis_index("ref")
    return j < 8, (j % 8 == 0) & (jnp.arange(KY_DEV) == 0)


def folded_references(references, spectral_weight):
    refs = references.shape[0]
    weighted = (spectral_weight[None, :, None, :] * references.astype(f32)).astype(bf16)
    weighted = weighted.reshape(refs, BOX, 2, KY_DEV, BOX)
    other = minus_kx(minus_index(mirrored(weighted, 3), 1))
    weighted = weighted.astype(f32)
    real = weighted[:, :, 0] + other[:, :, 0]
    imag = weighted[:, :, 1] - other[:, :, 1]
    real_0, real_32 = real[..., 0], real[..., HALF]
    imag_0, imag_32 = imag[..., 0], imag[..., HALF]
    lower, packed = column_kinds()
    real_end = jnp.where(lower, real_0, real_32)
    real_end = jnp.where(packed, 0.5 * (real_0 - imag_32), real_end)
    imag_end = jnp.where(lower, imag_0, imag_32)
    imag_end = jnp.where(packed, 0.5 * (imag_0 + real_32), imag_end)
    first = jnp.arange(HALF) == 0
    real_half = jnp.where(first, real_end[..., None], real[..., :HALF])
    imag_half = jnp.where(first, imag_end[..., None], imag[..., :HALF])
    both = jnp.stack([real_half, imag_half], axis=1)
    return both.reshape(refs, 128, 128)


def product_weights(spectral_weight):
    ends = spectral_weight[:, : HALF + 1 : HALF]
    ends = ends + minus_index(ends, 0)
    _, packed = column_kinds()
    cross = jnp.where(packed[0], 0.25 * (ends[:, :1] - ends[:, 1:]), 0.0)
    return jnp.tile(jnp.where(jnp.arange(128) == 0, cross, 0.0), (2, 1))


def square_weights(spectral_weight):
    near, far = to_near(spectral_weight), to_far(spectral_weight)
    partner = jnp.where(jnp.arange(4 * BOX) < BOX, near, far)
    order, depth = np.zeros((KY_DEV, BOX, KY_DEV, BOX), np.float32), np.zeros((BOX, BOX), np.float32)
    for k in range(BOX):
        depth[k, -k % BOX] = 1.0
        for kyl in range(KY_DEV):
            order[kyl, -k % BOX, -kyl % KY_DEV, k] = 1.0
    highest = lax.Precision.HIGHEST
    other = jnp.dot(jnp.asarray(depth), partner, precision=highest)
    other = jnp.dot(other, jnp.asarray(order.reshape(256, 256)), precision=highest)
    fold = (spectral_weight + other).reshape(BOX, KY_DEV, BOX)
    fold_0, fold_32 = fold[..., 0], fold[..., HALF]
    lower, packed = column_kinds()
    end = jnp.where(packed, 0.25 * (fold_0 + fold_32), jnp.where(lower, fold_0, fold_32))
    first = jnp.arange(HALF) == 0
    squares = jnp.where(first, end[..., None], fold[..., :HALF]).reshape(BOX, 128)
    return jnp.tile(squares, (2, 1))


def body(particles, counts, block_of, ref_index, references, spectral_weight):
    tomograms = lax.axis_size("tomo")
    rows = particles.shape[0]
    slots = 2 * tomograms
    refs = references.shape[0]
    positions = jnp.arange(rows, dtype=jnp.int32)

    is_live = positions < counts[0]
    same = (block_of[:, None] == block_of[None, :]) & is_live[:, None]
    before = positions[:, None] < positions[None, :]
    rank = jnp.sum((same & before).astype(jnp.int32), axis=0)
    slot_of = jnp.where(is_live, 2 * block_of + rank, slots)

    planes = half_planes(particles)
    pencils = lax.all_to_all(planes, "ref", split_axis=0, concat_axis=0, tiled=True)
    outgoing = half_spectra(
        slot_of, ref_index, pencils, product_weights(spectral_weight), slots
    )
    arrived = lax.all_to_all(outgoing, "tomo", split_axis=0, concat_axis=0, tiled=True)
    coefficients, table = lax.optimization_barrier(
        (folded_references(references, spectral_weight), table_of_device())
    )

    numbers = arrived[:, 32, 3::4, 0].reshape(slots)
    slot_index = numbers.astype(jnp.int32) - 1
    filled = slot_index >= 0
    slot_index = jnp.maximum(slot_index, 0)
    partial = jnp.sum(match(slot_index, arrived, coefficients, square_weights(spectral_weight)), axis=2)
    spread = jnp.broadcast_to(partial.reshape(1, 1, 2 * slots), (16, 1, 2 * slots))
    gathered = lax.all_to_all(spread, "ref", split_axis=0, concat_axis=0, tiled=True)
    totals = jnp.sum(gathered, axis=(0, 1)).reshape(2, slots)
    particle_norm = jnp.sqrt(totals[1] / float(BOX) ** 3 + 1e-05)
    slot_scores = jnp.where(filled, totals[0] / (float(BOX) ** 1.5 * particle_norm), 0.0)
    gain = jnp.where(filled, jax.nn.sigmoid(slot_scores) / particle_norm, 0.0)
    gain = gain.astype(bf16).astype(f32)

    returned = lax.all_to_all(
        slot_scores.reshape(tomograms, 1, 2), "tomo", split_axis=0, concat_axis=0, tiled=True
    )
    half, half_sent = insert(slot_index, gain, arrived, refs)
    reconstruction = unfold(half, to_near(half_sent), to_far(half_sent), table)
    returned, reconstruction = lax.optimization_barrier((returned, reconstruction))

    slot_ids = jnp.arange(slots, dtype=jnp.int32).reshape(tomograms, 1, 2, 1)
    row_scores = jnp.sum(jnp.where(slot_of == slot_ids, returned[..., None], 0.0), axis=(0, 1, 2))
    return (row_scores, reconstruction)


def solution(mesh):
    placed = (
        P("tomo", "ref", None),
        P("tomo"),
        P("tomo"),
        P("tomo"),
        P("tomo", None, None, "ref"),
        P(None, "ref"),
    )
    return jax.shard_map(
        body,
        mesh=mesh,
        in_specs=placed,
        out_specs=(P("tomo"), P("tomo", None, None, "ref")),
        check_vma=False,
    )
```

```python
import numpy as np

import jax
import jax.numpy as jnp
import ml_dtypes
from jax import lax
from jax.experimental import pallas as pl
from jax.experimental.pallas import tpu as pltpu
from jax.sharding import PartitionSpec as P

BOX = 64
HALF = 32
KY_DEV = 4
f32 = jnp.float32
bf16 = jnp.bfloat16


def split_hi_lo(table):
    high = table.astype(np.float32).astype(ml_dtypes.bfloat16)
    low = (table - high.astype(np.float64)).astype(np.float32).astype(ml_dtypes.bfloat16)
    return high, low


def angles(a, b):
    return 2.0 * np.pi / BOX * (np.outer(a, b) % BOX)


def x_table():
    x = np.arange(BOX)
    phase = angles(x, np.arange(HALF))
    real, imag = np.cos(phase), -np.sin(phase)
    imag[:, 0] = np.cos(np.pi * x)
    one = np.concatenate([real, imag, imag, -real], axis=1)
    table = np.zeros((2, BOX, 2, 4 * HALF))
    table[0, :, 0], table[1, :, 1] = one, one
    return np.concatenate(split_hi_lo(table.reshape(2 * BOX, 8 * HALF)), axis=0)


def y_table():
    rows = np.arange(BOX)
    ky = KY_DEV * (rows % 16) + rows // 16
    y = np.concatenate([np.arange(0, BOX, 2), np.arange(1, BOX, 2)])
    cosine, sine = np.cos(angles(ky, y)), np.sin(angles(ky, y))
    zero = np.zeros_like(cosine)
    plain = np.concatenate([cosine, sine], axis=1)
    lower = ky[:, None] < 32
    packed = ky[:, None] % 32 == 0
    real = np.where(lower, np.concatenate([cosine, zero], 1), np.concatenate([zero, cosine], 1))
    imag = np.where(lower, np.concatenate([zero, sine], 1), np.concatenate([-sine, zero], 1))
    real, imag = np.where(packed, plain, real), np.where(packed, plain, imag)
    high, low = split_hi_lo(np.concatenate([plain, real, imag], axis=0))
    return np.concatenate(
        [
            np.concatenate([high, high], axis=1),
            np.concatenate([low, np.zeros_like(low)], axis=1),
        ],
        axis=0,
    )


def z_table():
    phase = angles(np.arange(BOX), np.arange(BOX))
    table = np.zeros((2, BOX, BOX, 2))
    table[0, :, :, 0], table[0, :, :, 1] = np.cos(phase), np.sin(phase)
    table[1, :, :, 0], table[1, :, :, 1] = -np.sin(phase), np.cos(phase)
    return np.concatenate(split_hi_lo(table.reshape(2 * BOX, 2 * BOX)), axis=1)


def reverse_table():
    reverse = np.zeros((2, BOX, 2, BOX))
    for kz in range(BOX):
        reverse[0, kz, 0, -kz % BOX], reverse[1, kz, 1, -kz % BOX] = 1.0, -1.0
    return reverse.reshape(2 * BOX, 2 * BOX).astype(ml_dtypes.bfloat16)


def unfold_table(j):
    own, mirror = np.zeros((KY_DEV, HALF, KY_DEV, BOX)), np.zeros((KY_DEV, HALF, KY_DEV, BOX))
    own_turned, mirror_turned = np.zeros_like(own), np.zeros_like(own)
    here, there = (0, HALF) if j < 8 else (HALF, 0)
    for kyl in range(KY_DEV):
        to = (KY_DEV - kyl) % KY_DEV
        if kyl == 0 and j % 8 == 0:
            own[0, 0, 0, 0] = mirror[0, 0, 0, 0] = 0.5
            own_turned[0, 0, 0, HALF], mirror_turned[0, 0, 0, HALF] = 0.5, -0.5
        else:
            own[kyl, 0, kyl, here] = mirror[kyl, 0, to, there] = 1.0
        for kx in range(1, HALF):
            own[kyl, kx, kyl, kx] = mirror[kyl, kx, to, BOX - kx] = 1.0
    stacked = np.concatenate([own, own, mirror, own_turned, own_turned, mirror_turned], axis=0)
    return stacked.reshape(6 * 2 * BOX, 4 * BOX).astype(ml_dtypes.bfloat16)


def table_of_device():
    j = lax.axis_index("ref")
    kind = jnp.where(j % 8 == 0, 2, 0) + jnp.where(j < 8, 0, 1)
    kinds = jnp.asarray(np.stack([unfold_table(k) for k in (1, 9, 0, 8)]))
    return lax.dynamic_index_in_dim(kinds, kind, keepdims=False)


def params(mebibytes=40):
    return pltpu.CompilerParams(vmem_limit_bytes=mebibytes * 2**20)


def cost(microseconds):
    return pl.CostEstimate(
        flops=0, bytes_accessed=int(microseconds * 3.0e6), transcendentals=0
    )


def dot(a, b):
    return jnp.dot(a, b, preferred_element_type=f32)


def planes_kernel(x_ref, table_ref, out_ref, rows_buf, turn_buf):
    lane = lax.broadcasted_iota(jnp.int32, (1, 128), 1)
    low_half = lane < 64
    even = lane % 64 < 32
    wide_lane = lax.broadcasted_iota(jnp.int32, (1, 256), 1) % 64
    group = x_ref.shape[0]
    for row in range(group):
        volume = x_ref[row].astype(f32)
        for yt in range(32):
            start = 256 * row + 8 * yt
            rows_buf[start : start + 4, :] = volume[:, yt * 128 : (yt + 1) * 128]
    x = jnp.concatenate(
        [
            rows_buf[pl.ds(256 * row + zl, 32, stride=8), :]
            for row in range(group)
            for zl in range(4)
        ],
        axis=0,
    ).astype(bf16)
    along = dot(jnp.concatenate([x, x], axis=1), table_ref[:256])
    for row in range(group):
        tiles = []
        for zp in range(2):
            first, second = [], []
            start = 128 * row + 64 * zp
            for h in range(2):
                a = along[start : start + 32, 128 * h : 128 * h + 128]
                b = along[start + 32 : start + 64, 128 * h : 128 * h + 128]
                first.append(jnp.where(low_half, a, pltpu.roll(b, 64, 1)))
                second.append(jnp.where(low_half, pltpu.roll(a, 64, 1), b))
            tiles.append(jnp.concatenate(first + second, axis=0))
        wide = jnp.concatenate(tiles, axis=1)
        high = wide.astype(bf16)
        low = (wide - high.astype(f32)).astype(bf16)
        full = dot(table_ref[256:], jnp.concatenate([high, low], axis=0))
        full = full[:192] + full[192:]
        planes = jnp.where(wide_lane == 0, full[64:128], full[:64])
        planes = jnp.where(wide_lane == 32, full[128:], planes)
        for zp in range(2):
            i0, i1, i2, i3 = (
                planes[16 * k : 16 * k + 16, 128 * zp : 128 * zp + 128] for k in range(4)
            )
            p0 = jnp.where(low_half, i0, pltpu.roll(i2, 64, 1))
            p2 = jnp.where(low_half, pltpu.roll(i0, 64, 1), i2)
            p1 = jnp.where(low_half, i1, pltpu.roll(i3, 64, 1))
            p3 = jnp.where(low_half, pltpu.roll(i1, 64, 1), i3)
            turned = (
                jnp.where(even, p0, pltpu.roll(p1, 32, 1)),
                jnp.where(even, pltpu.roll(p0, 96, 1), p1),
                jnp.where(even, p2, pltpu.roll(p3, 32, 1)),
                jnp.where(even, pltpu.roll(p2, 96, 1), p3),
            )
            for g in range(4):
                start = 128 * row + (4 * zp + g) * 16
                turn_buf[start : start + 16, :] = turned[g]
    for pair in range(group // 2):
        for j in range(16):
            both = [turn_buf[pl.ds(128 * (2 * pair + e) + j, 8, stride=16), :] for e in range(2)]
            out_ref[j, pair] = jnp.concatenate(both, axis=0).astype(bf16)


def half_planes(particles):
    rows = particles.shape[0]
    group = 16
    return pl.pallas_call(
        planes_kernel,
        grid=(rows // group,),
        in_specs=[
            pl.BlockSpec((group, 4, BOX * BOX), lambda i: (i, 0, 0)),
            pl.BlockSpec((640, 256), lambda i: (0, 0)),
        ],
        out_specs=pl.BlockSpec((16, group // 2, 16, 128), lambda i: (0, i, 0, 0)),
        out_shape=jax.ShapeDtypeStruct((16, rows // 2, 16, 128), bf16),
        scratch_shapes=[
            pltpu.VMEM((group * 256, 128), f32),
            pltpu.VMEM((group * 128, 128), f32),
        ],
        compiler_params=params(58),
        cost_estimate=cost(8.0),
        name="half_planes",
    )(particles, jnp.asarray(np.concatenate([x_table(), y_table()], axis=0)))


def depth_kernel(slot_ref, index_ref, b_ref, table_ref, weight_ref, send_ref, *scratch):
    spec_buf, extra_buf, packed_buf, sems = scratch
    slots = extra_buf.shape[0]
    tomograms = slots // 2
    together = 16
    line = lax.broadcasted_iota(jnp.int32, (4, 128), 0)
    extra_buf[...] = jnp.zeros_like(extra_buf)
    weight = jnp.concatenate([weight_ref[...], weight_ref[...]], axis=0)

    def routed(row):
        slot = slot_ref[row]
        target = send_ref.at[slot // 2, pl.ds(16 * (slot % 2), 16)]
        return slot, pltpu.make_async_copy(spec_buf.at[row], target, sems.at[row])

    def step(i, _):
        done = []
        for p in range(together):
            block = b_ref[:, together * i + p].astype(f32)
            a = block[:, :8, :].reshape(128, 128)
            b = block[:, 8:, :].reshape(128, 128)
            pencils = jnp.concatenate([a, b], axis=1).astype(bf16)
            exact = dot(table_ref[:128], jnp.concatenate([pencils, pencils], axis=0))
            spectra = exact.astype(bf16)
            turned = dot(table_ref[128:, :128], spectra)
            for e in range(2):
                row = 2 * (together * i + p) + e
                one = exact[:, 128 * e : 128 * e + 128]
                spec_buf[row] = one.reshape(16, 8, 128).astype(bf16)
                terms = turned[:, 128 * e : 128 * e + 128] * weight
                value = spectra[:, 128 * e : 128 * e + 128].astype(f32)
                cross = jnp.sum(value * terms, axis=0, keepdims=True)
                high = cross.astype(bf16).astype(f32)
                middle = (cross - high).astype(bf16).astype(f32)
                low = cross - high - middle
                number = (index_ref[row] + 1).astype(f32)
                extra = jnp.where(line == 0, high, jnp.where(line == 1, middle, low))
                extra = jnp.where(line == 3, number, extra)
                done.append(extra)

        for r in range(2 * together):
            slot, copy = routed(2 * together * i + r)

            @pl.when(slot < slots)
            def _():
                copy.start()
                extra_buf[slot] = done[r]

        return 0

    lax.fori_loop(0, b_ref.shape[1] // together, step, 0)

    for t in range(tomograms):
        both = jnp.concatenate([extra_buf[2 * t], extra_buf[2 * t + 1]], axis=0)
        packed_buf[t] = both.astype(bf16)
    last = pltpu.make_async_copy(packed_buf, send_ref.at[:, 32], sems.at[sems.shape[0] - 1])
    last.start()

    def finish(row, _):
        slot, copy = routed(row)

        @pl.when(slot < slots)
        def _():
            copy.wait()

        return 0

    lax.fori_loop(0, 2 * b_ref.shape[1], finish, 0)
    last.wait()


def half_spectra(slot_of, ref_index, pencils, weights, slots):
    vmem = pl.BlockSpec(memory_space=pltpu.VMEM)
    smem = pl.BlockSpec(memory_space=pltpu.SMEM)
    rows = 2 * pencils.shape[1]
    reverse = np.concatenate([reverse_table(), np.zeros_like(reverse_table())], axis=1)
    return pl.pallas_call(
        depth_kernel,
        in_specs=[smem, smem, vmem, vmem, vmem],
        out_specs=pl.BlockSpec(memory_space=pl.ANY),
        out_shape=jax.ShapeDtypeStruct((slots // 2, 33, 8, 128), bf16),
        scratch_shapes=[
            pltpu.VMEM((rows, 16, 8, 128), bf16),
            pltpu.VMEM((slots, 4, 128), f32),
            pltpu.VMEM((slots // 2, 8, 128), bf16),
            pltpu.SemaphoreType.DMA((rows + 1,)),
        ],
        compiler_params=params(58),
        cost_estimate=cost(4.0),
        name="half_spectra",
    )(slot_of, ref_index, pencils, jnp.asarray(np.concatenate([z_table(), reverse])), weights)


def match_kernel(spec_ref, coef_ref, weight_ref, out_ref):
    group = spec_ref.shape[0]
    for t in range(group):
        extra = spec_ref[t, 32].astype(f32)
        for k in range(2):
            s = 2 * t + k
            value = spec_ref[t, 16 * k : 16 * k + 16].astype(f32).reshape(128, 128)
            index = jnp.maximum(extra[4 * k + 3, 0].astype(jnp.int32) - 1, 0)
            product = value * coef_ref[index]
            out_ref[0, s : s + 1, :] = jnp.sum(product, axis=0, keepdims=True)
            squares = jnp.sum(value * value * weight_ref[...], axis=0, keepdims=True)
            parts = jnp.sum(extra[4 * k : 4 * k + 3], axis=0, keepdims=True)
            out_ref[1, s : s + 1, :] = squares + parts


def match(arrived, coefficients, weights):
    slots = 2 * arrived.shape[0]
    refs = coefficients.shape[0]
    group = min(16, slots // 2)
    return pl.pallas_call(
        match_kernel,
        grid=(slots // 2 // group,),
        in_specs=[
            pl.BlockSpec((group, 33, 8, 128), lambda i: (i, 0, 0, 0)),
            pl.BlockSpec((refs, 128, 128), lambda i: (0, 0, 0)),
            pl.BlockSpec((128, 128), lambda i: (0, 0)),
        ],
        out_specs=pl.BlockSpec((2, 2 * group, 128), lambda i: (0, i, 0)),
        out_shape=jax.ShapeDtypeStruct((2, slots, 128), f32),
        compiler_params=params(),
        cost_estimate=cost(2.0),
        name="match",
    )(arrived, coefficients, weights)


def insert_kernel(index_ref, gain_ref, spec_ref, out_ref, sent_ref):
    group = spec_ref.shape[0]
    step = pl.program_id(0)

    @pl.when(step == 0)
    def _():
        out_ref[...] = jnp.zeros_like(out_ref)

    for t in range(group):
        for k in range(2):
            slot = step * 2 * group + 2 * t + k
            value = spec_ref[t, 16 * k : 16 * k + 16].astype(f32).reshape(128, 128)
            gain = gain_ref[slot]
            out_ref[index_ref[slot]] += jnp.where(gain > 0.0, gain * value, 0.0)

    @pl.when(step == pl.num_programs(0) - 1)
    def _():
        sent_ref[...] = out_ref[...].astype(bf16)


def insert(index, gain, arrived, refs):
    slots = index.shape[0]
    group = min(4, slots // 2)
    whole = pl.BlockSpec((refs, 128, 128), lambda i, *_: (0, 0, 0))
    return pl.pallas_call(
        insert_kernel,
        grid_spec=pltpu.PrefetchScalarGridSpec(
            num_scalar_prefetch=2,
            grid=(slots // 2 // group,),
            in_specs=[pl.BlockSpec((group, 33, 8, 128), lambda i, *_: (i, 0, 0, 0))],
            out_specs=[whole, whole],
        ),
        out_shape=[
            jax.ShapeDtypeStruct((refs, 128, 128), f32),
            jax.ShapeDtypeStruct((refs, 128, 128), bf16),
        ],
        compiler_params=params(),
        cost_estimate=cost(25.0),
        name="insert",
    )(index, gain, arrived)


def unfold_kernel(own_ref, near_ref, far_ref, q_ref, reverse_ref, out_ref):
    lane = lax.broadcasted_iota(jnp.int32, (1, 128), 1)
    own = own_ref[...]
    partner = jnp.where(lane < HALF, near_ref[...].astype(f32), far_ref[...].astype(f32)).astype(bf16)
    conjugate = dot(reverse_ref[...], partner)

    def turned(v):
        return jnp.concatenate([v[64:], -v[:64]], axis=0)

    high = own.astype(bf16).astype(f32)
    parts = [high, own - high, conjugate]
    parts = parts + [turned(v) for v in parts]
    full = dot(jnp.concatenate(parts, axis=1).astype(bf16), q_ref[...])
    for lt in range(2):
        for c in range(2):
            out_ref[pl.ds(2 * lt + c, 64, stride=4), :] = full[
                64 * c : 64 * c + 64, 128 * lt : 128 * lt + 128
            ]


def unfold(own, near, far, table):
    refs = own.shape[0]
    one = pl.BlockSpec((None, 128, 128), lambda i: (i, 0, 0))
    packed = pl.pallas_call(
        unfold_kernel,
        grid=(refs,),
        in_specs=[
            one,
            one,
            one,
            pl.BlockSpec((768, 256), lambda i: (0, 0)),
            pl.BlockSpec((128, 128), lambda i: (0, 0)),
        ],
        out_specs=pl.BlockSpec((None, 256, 128), lambda i: (i, 0, 0)),
        out_shape=jax.ShapeDtypeStruct((refs, 256, 128), f32),
        compiler_params=params(),
        cost_estimate=cost(0.5),
        name="unfold",
    )(own, near, far, table, jnp.asarray(reverse_table()))
    tiles = packed.reshape(refs, BOX, 2, 2, 128)
    return tiles.transpose(0, 1, 3, 2, 4).reshape(refs, BOX, 2, 256)


def to_far(values):
    return lax.ppermute(values, "ref", [(j, 15 - j) for j in range(16)])


def to_near(values):
    return lax.ppermute(values, "ref", [(j, -j % 16) for j in range(16)])


def mirrored(values, ky_axis):
    near = to_near(lax.slice_in_dim(values, 0, 1, axis=ky_axis))
    far = to_far(lax.slice_in_dim(values, 1, KY_DEV, axis=ky_axis))
    return jnp.concatenate([near, lax.rev(far, (ky_axis,))], axis=ky_axis)


def minus_index(values, axis):
    return jnp.roll(lax.rev(values, (axis,)), 1, axis)


def minus_kx(values):
    order = np.zeros((BOX, BOX), np.float32)
    for kx in range(BOX):
        order[-kx % BOX, kx] = 1.0
    return jnp.einsum(
        "...x,xk->...k", values, jnp.asarray(order, values.dtype), precision=lax.Precision.HIGHEST,
        preferred_element_type=f32,
    )


def column_kinds():
    j = lax.axis_index("ref")
    return j < 8, (j % 8 == 0) & (jnp.arange(KY_DEV) == 0)


def folded_references(references, spectral_weight):
    refs = references.shape[0]
    weighted = (spectral_weight[None, :, None, :] * references.astype(f32)).astype(bf16)
    weighted = weighted.reshape(refs, BOX, 2, KY_DEV, BOX)
    other = minus_kx(minus_index(mirrored(weighted, 3), 1))
    weighted = weighted.astype(f32)
    real = weighted[:, :, 0] + other[:, :, 0]
    imag = weighted[:, :, 1] - other[:, :, 1]
    real_0, real_32 = real[..., 0], real[..., HALF]
    imag_0, imag_32 = imag[..., 0], imag[..., HALF]
    lower, packed = column_kinds()
    real_end = jnp.where(lower, real_0, real_32)
    real_end = jnp.where(packed, 0.5 * (real_0 - imag_32), real_end)
    imag_end = jnp.where(lower, imag_0, imag_32)
    imag_end = jnp.where(packed, 0.5 * (imag_0 + real_32), imag_end)
    first = jnp.arange(HALF) == 0
    real_half = jnp.where(first, real_end[..., None], real[..., :HALF])
    imag_half = jnp.where(first, imag_end[..., None], imag[..., :HALF])
    both = jnp.stack([real_half, imag_half], axis=1)
    return both.reshape(refs, 128, 128)


def product_weights(spectral_weight):
    ends = spectral_weight[:, : HALF + 1 : HALF]
    ends = ends + minus_index(ends, 0)
    _, packed = column_kinds()
    cross = jnp.where(packed[0], 0.25 * (ends[:, :1] - ends[:, 1:]), 0.0)
    return jnp.where(jnp.arange(128) == 0, cross, 0.0)


def square_weights(spectral_weight):
    near, far = to_near(spectral_weight), to_far(spectral_weight)
    partner = jnp.where(jnp.arange(4 * BOX) < BOX, near, far)
    order, depth = np.zeros((KY_DEV, BOX, KY_DEV, BOX), np.float32), np.zeros((BOX, BOX), np.float32)
    for k in range(BOX):
        depth[k, -k % BOX] = 1.0
        for kyl in range(KY_DEV):
            order[kyl, -k % BOX, -kyl % KY_DEV, k] = 1.0
    highest = lax.Precision.HIGHEST
    other = jnp.dot(jnp.asarray(depth), partner, precision=highest)
    other = jnp.dot(other, jnp.asarray(order.reshape(256, 256)), precision=highest)
    fold = (spectral_weight + other).reshape(BOX, KY_DEV, BOX)
    fold_0, fold_32 = fold[..., 0], fold[..., HALF]
    lower, packed = column_kinds()
    end = jnp.where(packed, 0.25 * (fold_0 + fold_32), jnp.where(lower, fold_0, fold_32))
    first = jnp.arange(HALF) == 0
    squares = jnp.where(first, end[..., None], fold[..., :HALF]).reshape(BOX, 128)
    return jnp.tile(squares, (2, 1))


def body(particles, counts, block_of, ref_index, references, spectral_weight):
    tomograms = lax.axis_size("tomo")
    rows = particles.shape[0]
    slots = 2 * tomograms
    refs = references.shape[0]
    positions = jnp.arange(rows, dtype=jnp.int32)

    is_live = positions < counts[0]
    same = (block_of[:, None] == block_of[None, :]) & is_live[:, None]
    before = positions[:, None] < positions[None, :]
    rank = jnp.sum((same & before).astype(jnp.int32), axis=0)
    slot_of = jnp.where(is_live, 2 * block_of + rank, slots)

    planes = half_planes(particles)
    pencils = lax.all_to_all(planes, "ref", split_axis=0, concat_axis=0, tiled=True)
    outgoing = half_spectra(
        slot_of, ref_index, pencils, product_weights(spectral_weight), slots
    )
    arrived = lax.all_to_all(outgoing, "tomo", split_axis=0, concat_axis=0, tiled=True)
    coefficients, table = lax.optimization_barrier(
        (folded_references(references, spectral_weight), table_of_device())
    )

    numbers = arrived[:, 32, 3::4, 0].reshape(slots)
    slot_index = numbers.astype(jnp.int32) - 1
    filled = slot_index >= 0
    slot_index = jnp.maximum(slot_index, 0)
    partial = jnp.sum(match(arrived, coefficients, square_weights(spectral_weight)), axis=2)
    spread = jnp.broadcast_to(partial.reshape(1, 1, 2 * slots), (16, 1, 2 * slots))
    gathered = lax.all_to_all(spread, "ref", split_axis=0, concat_axis=0, tiled=True)
    totals = jnp.sum(gathered, axis=(0, 1)).reshape(2, slots)
    particle_norm = jnp.sqrt(totals[1] / float(BOX) ** 3 + 1e-05)
    slot_scores = jnp.where(filled, totals[0] / (float(BOX) ** 1.5 * particle_norm), 0.0)
    gain = jnp.where(filled, jax.nn.sigmoid(slot_scores) / particle_norm, 0.0)
    gain = gain.astype(bf16).astype(f32)

    returned = lax.all_to_all(
        slot_scores.reshape(tomograms, 1, 2), "tomo", split_axis=0, concat_axis=0, tiled=True
    )
    half, half_sent = insert(slot_index, gain, arrived, refs)
    reconstruction = unfold(half, to_near(half_sent), to_far(half_sent), table)
    returned, reconstruction = lax.optimization_barrier((returned, reconstruction))

    slot_ids = jnp.arange(slots, dtype=jnp.int32).reshape(tomograms, 1, 2, 1)
    row_scores = jnp.sum(jnp.where(slot_of == slot_ids, returned[..., None], 0.0), axis=(0, 1, 2))
    return (row_scores, reconstruction)


def solution(mesh):
    placed = (
        P("tomo", "ref", None),
        P("tomo"),
        P("tomo"),
        P("tomo"),
        P("tomo", None, None, "ref"),
        P(None, "ref"),
    )
    return jax.shard_map(
        body,
        mesh=mesh,
        in_specs=placed,
        out_specs=(P("tomo"), P("tomo", None, None, "ref")),
        check_vma=False,
    )
```

```python
import numpy as np

import jax
import jax.numpy as jnp
import ml_dtypes
from jax import lax
from jax.experimental import pallas as pl
from jax.experimental.pallas import tpu as pltpu
from jax.sharding import PartitionSpec as P

BOX = 64
HALF = 32
KY_DEV = 4
f32 = jnp.float32
bf16 = jnp.bfloat16


def split_hi_lo(table):
    high = table.astype(np.float32).astype(ml_dtypes.bfloat16)
    low = (table - high.astype(np.float64)).astype(np.float32).astype(ml_dtypes.bfloat16)
    return high, low


def angles(a, b):
    return 2.0 * np.pi / BOX * (np.outer(a, b) % BOX)


def x_table():
    x = np.arange(BOX)
    phase = angles(x, np.arange(HALF))
    real, imag = np.cos(phase), -np.sin(phase)
    imag[:, 0] = np.cos(np.pi * x)
    one = np.concatenate([real, imag, imag, -real], axis=1)
    table = np.zeros((2, BOX, 2, 4 * HALF))
    table[0, :, 0], table[1, :, 1] = one, one
    return np.concatenate(split_hi_lo(table.reshape(2 * BOX, 8 * HALF)), axis=0)


def y_table():
    rows = np.arange(BOX)
    ky = KY_DEV * (rows % 16) + rows // 16
    y = np.concatenate([np.arange(0, BOX, 2), np.arange(1, BOX, 2)])
    cosine, sine = np.cos(angles(ky, y)), np.sin(angles(ky, y))
    zero = np.zeros_like(cosine)
    plain = np.concatenate([cosine, sine], axis=1)
    lower = ky[:, None] < 32
    packed = ky[:, None] % 32 == 0
    real = np.where(lower, np.concatenate([cosine, zero], 1), np.concatenate([zero, cosine], 1))
    imag = np.where(lower, np.concatenate([zero, sine], 1), np.concatenate([-sine, zero], 1))
    real, imag = np.where(packed, plain, real), np.where(packed, plain, imag)
    high, low = split_hi_lo(np.concatenate([plain, real, imag], axis=0))
    return np.concatenate(
        [
            np.concatenate([high, high], axis=1),
            np.concatenate([low, np.zeros_like(low)], axis=1),
        ],
        axis=0,
    )


def z_table():
    phase = angles(np.arange(BOX), np.arange(BOX))
    table = np.zeros((2, BOX, BOX, 2))
    table[0, :, :, 0], table[0, :, :, 1] = np.cos(phase), np.sin(phase)
    table[1, :, :, 0], table[1, :, :, 1] = -np.sin(phase), np.cos(phase)
    return np.concatenate(split_hi_lo(table.reshape(2 * BOX, 2 * BOX)), axis=1)


def reverse_table():
    reverse = np.zeros((2, BOX, 2, BOX))
    for kz in range(BOX):
        reverse[0, kz, 0, -kz % BOX], reverse[1, kz, 1, -kz % BOX] = 1.0, -1.0
    return reverse.reshape(2 * BOX, 2 * BOX).astype(ml_dtypes.bfloat16)


def unfold_table(j):
    own, mirror = np.zeros((KY_DEV, HALF, KY_DEV, BOX)), np.zeros((KY_DEV, HALF, KY_DEV, BOX))
    own_turned, mirror_turned = np.zeros_like(own), np.zeros_like(own)
    here, there = (0, HALF) if j < 8 else (HALF, 0)
    for kyl in range(KY_DEV):
        to = (KY_DEV - kyl) % KY_DEV
        if kyl == 0 and j % 8 == 0:
            own[0, 0, 0, 0] = mirror[0, 0, 0, 0] = 0.5
            own_turned[0, 0, 0, HALF], mirror_turned[0, 0, 0, HALF] = 0.5, -0.5
        else:
            own[kyl, 0, kyl, here] = mirror[kyl, 0, to, there] = 1.0
        for kx in range(1, HALF):
            own[kyl, kx, kyl, kx] = mirror[kyl, kx, to, BOX - kx] = 1.0
    stacked = np.concatenate([own, own, mirror, own_turned, own_turned, mirror_turned], axis=0)
    return stacked.reshape(6 * 2 * BOX, 4 * BOX).astype(ml_dtypes.bfloat16)


def table_of_device():
    j = lax.axis_index("ref")
    kind = jnp.where(j % 8 == 0, 2, 0) + jnp.where(j < 8, 0, 1)
    kinds = jnp.asarray(np.stack([unfold_table(k) for k in (1, 9, 0, 8)]))
    return lax.dynamic_index_in_dim(kinds, kind, keepdims=False)


def params(mebibytes=40):
    return pltpu.CompilerParams(vmem_limit_bytes=mebibytes * 2**20)


def cost(microseconds):
    return pl.CostEstimate(
        flops=0, bytes_accessed=int(microseconds * 3.0e6), transcendentals=0
    )


def dot(a, b):
    return jnp.dot(a, b, preferred_element_type=f32)


def planes_kernel(x_ref, table_ref, out_ref, rows_buf, turn_buf):
    lane = lax.broadcasted_iota(jnp.int32, (1, 128), 1)
    low_half = lane < 64
    even = lane % 64 < 32
    wide_lane = lax.broadcasted_iota(jnp.int32, (1, 256), 1) % 64
    group = x_ref.shape[0]
    for row in range(group):
        volume = x_ref[row].astype(f32)
        for yt in range(32):
            start = 256 * row + 8 * yt
            rows_buf[start : start + 4, :] = volume[:, yt * 128 : (yt + 1) * 128]
    x = jnp.concatenate(
        [
            rows_buf[pl.ds(256 * row + zl, 32, stride=8), :]
            for row in range(group)
            for zl in range(4)
        ],
        axis=0,
    ).astype(bf16)
    along = dot(jnp.concatenate([x, x], axis=1), table_ref[:256])
    for row in range(group):
        tiles = []
        for zp in range(2):
            first, second = [], []
            start = 128 * row + 64 * zp
            for h in range(2):
                a = along[start : start + 32, 128 * h : 128 * h + 128]
                b = along[start + 32 : start + 64, 128 * h : 128 * h + 128]
                first.append(jnp.where(low_half, a, pltpu.roll(b, 64, 1)))
                second.append(jnp.where(low_half, pltpu.roll(a, 64, 1), b))
            tiles.append(jnp.concatenate(first + second, axis=0))
        wide = jnp.concatenate(tiles, axis=1)
        high = wide.astype(bf16)
        low = (wide - high.astype(f32)).astype(bf16)
        full = dot(table_ref[256:], jnp.concatenate([high, low], axis=0))
        full = full[:192] + full[192:]
        planes = jnp.where(wide_lane == 0, full[64:128], full[:64])
        planes = jnp.where(wide_lane == 32, full[128:], planes)
        for zp in range(2):
            i0, i1, i2, i3 = (
                planes[16 * k : 16 * k + 16, 128 * zp : 128 * zp + 128] for k in range(4)
            )
            p0 = jnp.where(low_half, i0, pltpu.roll(i2, 64, 1))
            p2 = jnp.where(low_half, pltpu.roll(i0, 64, 1), i2)
            p1 = jnp.where(low_half, i1, pltpu.roll(i3, 64, 1))
            p3 = jnp.where(low_half, pltpu.roll(i1, 64, 1), i3)
            turned = (
                jnp.where(even, p0, pltpu.roll(p1, 32, 1)),
                jnp.where(even, pltpu.roll(p0, 96, 1), p1),
                jnp.where(even, p2, pltpu.roll(p3, 32, 1)),
                jnp.where(even, pltpu.roll(p2, 96, 1), p3),
            )
            for g in range(4):
                start = 128 * row + (4 * zp + g) * 16
                turn_buf[start : start + 16, :] = turned[g]
    for pair in range(group // 2):
        for j in range(16):
            both = [turn_buf[pl.ds(128 * (2 * pair + e) + j, 8, stride=16), :] for e in range(2)]
            out_ref[j, pair] = jnp.concatenate(both, axis=0).astype(bf16)


def half_planes(particles):
    rows = particles.shape[0]
    group = 16
    return pl.pallas_call(
        planes_kernel,
        grid=(rows // group,),
        in_specs=[
            pl.BlockSpec((group, 4, BOX * BOX), lambda i: (i, 0, 0)),
            pl.BlockSpec((640, 256), lambda i: (0, 0)),
        ],
        out_specs=pl.BlockSpec((16, group // 2, 16, 128), lambda i: (0, i, 0, 0)),
        out_shape=jax.ShapeDtypeStruct((16, rows // 2, 16, 128), bf16),
        scratch_shapes=[
            pltpu.VMEM((group * 256, 128), f32),
            pltpu.VMEM((group * 128, 128), f32),
        ],
        compiler_params=params(58),
        cost_estimate=cost(8.0),
        name="half_planes",
    )(particles, jnp.asarray(np.concatenate([x_table(), y_table()], axis=0)))


def depth_kernel(slot_ref, index_ref, b_ref, table_ref, weight_ref, send_ref, *scratch):
    spec_buf, extra_buf, packed_buf, sems = scratch
    slots = extra_buf.shape[0]
    tomograms = slots // 2
    together = 16
    line = lax.broadcasted_iota(jnp.int32, (4, 128), 0)
    extra_buf[...] = jnp.zeros_like(extra_buf)
    weight = jnp.concatenate([weight_ref[...], weight_ref[...]], axis=0)

    def routed(row):
        slot = slot_ref[row]
        target = send_ref.at[slot // 2, pl.ds(16 * (slot % 2), 16)]
        return slot, pltpu.make_async_copy(spec_buf.at[row], target, sems.at[row])

    def step(i, _):
        done = []
        for p in range(together):
            block = b_ref[:, together * i + p].astype(f32)
            a = block[:, :8, :].reshape(128, 128)
            b = block[:, 8:, :].reshape(128, 128)
            pencils = jnp.concatenate([a, b], axis=1).astype(bf16)
            exact = dot(table_ref[:128], jnp.concatenate([pencils, pencils], axis=0))
            spectra = exact.astype(bf16)
            turned = dot(table_ref[128:, :128], spectra)
            for e in range(2):
                row = 2 * (together * i + p) + e
                one = exact[:, 128 * e : 128 * e + 128]
                spec_buf[row] = one.reshape(16, 8, 128).astype(bf16)
                terms = turned[:, 128 * e : 128 * e + 128] * weight
                value = spectra[:, 128 * e : 128 * e + 128].astype(f32)
                cross = jnp.sum(value * terms, axis=0, keepdims=True)
                high = cross.astype(bf16).astype(f32)
                middle = (cross - high).astype(bf16).astype(f32)
                low = cross - high - middle
                number = (index_ref[row] + 1).astype(f32)
                extra = jnp.where(line == 0, high, jnp.where(line == 1, middle, low))
                extra = jnp.where(line == 3, number, extra)
                done.append(extra)

        for r in range(2 * together):
            slot, copy = routed(2 * together * i + r)

            @pl.when(slot < slots)
            def _():
                copy.start()
                extra_buf[slot] = done[r]

        return 0

    lax.fori_loop(0, b_ref.shape[1] // together, step, 0)

    for t in range(tomograms):
        both = jnp.concatenate([extra_buf[2 * t], extra_buf[2 * t + 1]], axis=0)
        packed_buf[t] = both.astype(bf16)
    last = pltpu.make_async_copy(packed_buf, send_ref.at[:, 32], sems.at[sems.shape[0] - 1])
    last.start()

    def finish(row, _):
        slot, copy = routed(row)

        @pl.when(slot < slots)
        def _():
            copy.wait()

        return 0

    lax.fori_loop(0, 2 * b_ref.shape[1], finish, 0)
    last.wait()


def half_spectra(slot_of, ref_index, pencils, weights, slots):
    vmem = pl.BlockSpec(memory_space=pltpu.VMEM)
    smem = pl.BlockSpec(memory_space=pltpu.SMEM)
    rows = 2 * pencils.shape[1]
    reverse = np.concatenate([reverse_table(), np.zeros_like(reverse_table())], axis=1)
    return pl.pallas_call(
        depth_kernel,
        in_specs=[smem, smem, vmem, vmem, vmem],
        out_specs=pl.BlockSpec(memory_space=pl.ANY),
        out_shape=jax.ShapeDtypeStruct((slots // 2, 33, 8, 128), bf16),
        scratch_shapes=[
            pltpu.VMEM((rows, 16, 8, 128), bf16),
            pltpu.VMEM((slots, 4, 128), f32),
            pltpu.VMEM((slots // 2, 8, 128), bf16),
            pltpu.SemaphoreType.DMA((rows + 1,)),
        ],
        compiler_params=params(52),
        cost_estimate=cost(4.0),
        name="half_spectra",
    )(slot_of, ref_index, pencils, jnp.asarray(np.concatenate([z_table(), reverse])), weights)


def match_kernel(spec_ref, coef_ref, weight_ref, out_ref, sums_buf):
    tomograms = spec_ref.shape[0]
    for t in range(tomograms):
        extra = spec_ref[t, 32].astype(f32)
        for k in range(2):
            slot = 2 * t + k
            value = spec_ref[t, 16 * k : 16 * k + 16].astype(f32).reshape(128, 128)
            index = jnp.maximum(extra[4 * k + 3, 0].astype(jnp.int32) - 1, 0)
            product = value * coef_ref[index]
            squares = jnp.sum(value * value * weight_ref[...], axis=0, keepdims=True)
            parts = jnp.sum(extra[4 * k : 4 * k + 3], axis=0, keepdims=True)
            row = 2 * tomograms + slot
            sums_buf[slot : slot + 1, :] = jnp.sum(product, axis=0, keepdims=True)
            sums_buf[row : row + 1, :] = squares + parts
    totals = jnp.sum(sums_buf[...].T, axis=0, keepdims=True)
    out_ref[...] = jnp.broadcast_to(totals[None], out_ref.shape)


def match(arrived, coefficients, weights):
    slots = 2 * arrived.shape[0]
    vmem = pl.BlockSpec(memory_space=pltpu.VMEM)
    return pl.pallas_call(
        match_kernel,
        in_specs=[vmem, vmem, vmem],
        out_specs=vmem,
        out_shape=jax.ShapeDtypeStruct((16, 1, 2 * slots), f32),
        scratch_shapes=[pltpu.VMEM((2 * slots, 128), f32)],
        compiler_params=params(),
        cost_estimate=cost(2.0),
        name="match",
    )(arrived, coefficients, weights)


def insert_kernel(index_ref, gain_ref, spec_ref, out_ref, sent_ref):
    group = spec_ref.shape[0]
    step = pl.program_id(0)

    @pl.when(step == 0)
    def _():
        out_ref[...] = jnp.zeros_like(out_ref)

    for t in range(group):
        for k in range(2):
            slot = step * 2 * group + 2 * t + k
            value = spec_ref[t, 16 * k : 16 * k + 16].astype(f32).reshape(128, 128)
            gain = gain_ref[slot]
            out_ref[index_ref[slot]] += jnp.where(gain > 0.0, gain * value, 0.0)

    @pl.when(step == pl.num_programs(0) - 1)
    def _():
        sent_ref[...] = out_ref[...].astype(bf16)


def insert(index, gain, arrived, refs):
    slots = index.shape[0]
    group = min(16, slots // 2)
    whole = pl.BlockSpec((refs, 128, 128), lambda i, *_: (0, 0, 0))
    return pl.pallas_call(
        insert_kernel,
        grid_spec=pltpu.PrefetchScalarGridSpec(
            num_scalar_prefetch=2,
            grid=(slots // 2 // group,),
            in_specs=[pl.BlockSpec((group, 33, 8, 128), lambda i, *_: (i, 0, 0, 0))],
            out_specs=[whole, whole],
        ),
        out_shape=[
            jax.ShapeDtypeStruct((refs, 128, 128), f32),
            jax.ShapeDtypeStruct((refs, 128, 128), bf16),
        ],
        compiler_params=params(),
        cost_estimate=cost(25.0),
        name="insert",
    )(index, gain, arrived)


def unfold_kernel(own_ref, near_ref, far_ref, q_ref, reverse_ref, out_ref):
    lane = lax.broadcasted_iota(jnp.int32, (1, 128), 1)
    own = own_ref[...]
    partner = jnp.where(lane < HALF, near_ref[...].astype(f32), far_ref[...].astype(f32)).astype(bf16)
    conjugate = dot(reverse_ref[...], partner)

    def turned(v):
        return jnp.concatenate([v[64:], -v[:64]], axis=0)

    high = own.astype(bf16).astype(f32)
    parts = [high, own - high, conjugate]
    parts = parts + [turned(v) for v in parts]
    full = dot(jnp.concatenate(parts, axis=1).astype(bf16), q_ref[...])
    for lt in range(2):
        for c in range(2):
            out_ref[pl.ds(2 * lt + c, 64, stride=4), :] = full[
                64 * c : 64 * c + 64, 128 * lt : 128 * lt + 128
            ]


def unfold(own, near, far, table):
    refs = own.shape[0]
    one = pl.BlockSpec((None, 128, 128), lambda i: (i, 0, 0))
    packed = pl.pallas_call(
        unfold_kernel,
        grid=(refs,),
        in_specs=[
            one,
            one,
            one,
            pl.BlockSpec((768, 256), lambda i: (0, 0)),
            pl.BlockSpec((128, 128), lambda i: (0, 0)),
        ],
        out_specs=pl.BlockSpec((None, 256, 128), lambda i: (i, 0, 0)),
        out_shape=jax.ShapeDtypeStruct((refs, 256, 128), f32),
        compiler_params=params(),
        cost_estimate=cost(0.5),
        name="unfold",
    )(own, near, far, table, jnp.asarray(reverse_table()))
    tiles = packed.reshape(refs, BOX, 2, 2, 128)
    return tiles.transpose(0, 1, 3, 2, 4).reshape(refs, BOX, 2, 256)


def to_far(values):
    return lax.ppermute(values, "ref", [(j, 15 - j) for j in range(16)])


def to_near(values):
    return lax.ppermute(values, "ref", [(j, -j % 16) for j in range(16)])


def mirrored(values, ky_axis):
    near = to_near(lax.slice_in_dim(values, 0, 1, axis=ky_axis))
    far = to_far(lax.slice_in_dim(values, 1, KY_DEV, axis=ky_axis))
    return jnp.concatenate([near, lax.rev(far, (ky_axis,))], axis=ky_axis)


def minus_index(values, axis):
    return jnp.roll(lax.rev(values, (axis,)), 1, axis)


def minus_kx(values):
    order = np.zeros((BOX, BOX), np.float32)
    for kx in range(BOX):
        order[-kx % BOX, kx] = 1.0
    return jnp.einsum(
        "...x,xk->...k", values, jnp.asarray(order, values.dtype), precision=lax.Precision.HIGHEST,
        preferred_element_type=f32,
    )


def column_kinds():
    j = lax.axis_index("ref")
    return j < 8, (j % 8 == 0) & (jnp.arange(KY_DEV) == 0)


def folded_references(references, spectral_weight):
    refs = references.shape[0]
    weighted = (spectral_weight[None, :, None, :] * references.astype(f32)).astype(bf16)
    weighted = weighted.reshape(refs, BOX, 2, KY_DEV, BOX)
    other = minus_kx(minus_index(mirrored(weighted, 3), 1))
    weighted = weighted.astype(f32)
    real = weighted[:, :, 0] + other[:, :, 0]
    imag = weighted[:, :, 1] - other[:, :, 1]
    real_0, real_32 = real[..., 0], real[..., HALF]
    imag_0, imag_32 = imag[..., 0], imag[..., HALF]
    lower, packed = column_kinds()
    real_end = jnp.where(lower, real_0, real_32)
    real_end = jnp.where(packed, 0.5 * (real_0 - imag_32), real_end)
    imag_end = jnp.where(lower, imag_0, imag_32)
    imag_end = jnp.where(packed, 0.5 * (imag_0 + real_32), imag_end)
    first = jnp.arange(HALF) == 0
    real_half = jnp.where(first, real_end[..., None], real[..., :HALF])
    imag_half = jnp.where(first, imag_end[..., None], imag[..., :HALF])
    both = jnp.stack([real_half, imag_half], axis=1)
    return both.reshape(refs, 128, 128)


def product_weights(spectral_weight):
    ends = spectral_weight[:, : HALF + 1 : HALF]
    ends = ends + minus_index(ends, 0)
    _, packed = column_kinds()
    cross = jnp.where(packed[0], 0.25 * (ends[:, :1] - ends[:, 1:]), 0.0)
    return jnp.where(jnp.arange(128) == 0, cross, 0.0)


def square_weights(spectral_weight):
    near, far = to_near(spectral_weight), to_far(spectral_weight)
    partner = jnp.where(jnp.arange(4 * BOX) < BOX, near, far)
    order, depth = np.zeros((KY_DEV, BOX, KY_DEV, BOX), np.float32), np.zeros((BOX, BOX), np.float32)
    for k in range(BOX):
        depth[k, -k % BOX] = 1.0
        for kyl in range(KY_DEV):
            order[kyl, -k % BOX, -kyl % KY_DEV, k] = 1.0
    highest = lax.Precision.HIGHEST
    other = jnp.dot(jnp.asarray(depth), partner, precision=highest)
    other = jnp.dot(other, jnp.asarray(order.reshape(256, 256)), precision=highest)
    fold = (spectral_weight + other).reshape(BOX, KY_DEV, BOX)
    fold_0, fold_32 = fold[..., 0], fold[..., HALF]
    lower, packed = column_kinds()
    end = jnp.where(packed, 0.25 * (fold_0 + fold_32), jnp.where(lower, fold_0, fold_32))
    first = jnp.arange(HALF) == 0
    squares = jnp.where(first, end[..., None], fold[..., :HALF]).reshape(BOX, 128)
    return jnp.tile(squares, (2, 1))


def body(particles, counts, block_of, ref_index, references, spectral_weight):
    tomograms = lax.axis_size("tomo")
    rows = particles.shape[0]
    slots = 2 * tomograms
    refs = references.shape[0]
    positions = jnp.arange(rows, dtype=jnp.int32)

    is_live = positions < counts[0]
    same = (block_of[:, None] == block_of[None, :]) & is_live[:, None]
    before = positions[:, None] < positions[None, :]
    rank = jnp.sum((same & before).astype(jnp.int32), axis=0)
    slot_of = jnp.where(is_live, 2 * block_of + rank, slots)

    planes = half_planes(particles)
    pencils = lax.all_to_all(planes, "ref", split_axis=0, concat_axis=0, tiled=True)
    outgoing = half_spectra(
        slot_of, ref_index, pencils, product_weights(spectral_weight), slots
    )
    arrived = lax.all_to_all(outgoing, "tomo", split_axis=0, concat_axis=0, tiled=True)
    coefficients, table = lax.optimization_barrier(
        (folded_references(references, spectral_weight), table_of_device())
    )

    numbers = arrived[:, 32, 3::4, 0].reshape(slots)
    slot_index = numbers.astype(jnp.int32) - 1
    filled = slot_index >= 0
    slot_index = jnp.maximum(slot_index, 0)
    spread = match(arrived, coefficients, square_weights(spectral_weight))
    gathered = lax.all_to_all(spread, "ref", split_axis=0, concat_axis=0, tiled=True)
    totals = jnp.sum(gathered, axis=(0, 1)).reshape(2, slots)
    particle_norm = jnp.sqrt(totals[1] / float(BOX) ** 3 + 1e-05)
    slot_scores = jnp.where(filled, totals[0] / (float(BOX) ** 1.5 * particle_norm), 0.0)
    gain = jnp.where(filled, jax.nn.sigmoid(slot_scores) / particle_norm, 0.0)
    gain = gain.astype(bf16).astype(f32)

    returned = lax.all_to_all(
        slot_scores.reshape(tomograms, 1, 2), "tomo", split_axis=0, concat_axis=0, tiled=True
    )
    half, half_sent = insert(slot_index, gain, arrived, refs)
    reconstruction = unfold(half, to_near(half_sent), to_far(half_sent), table)
    returned, reconstruction = lax.optimization_barrier((returned, reconstruction))

    slot_ids = jnp.arange(slots, dtype=jnp.int32).reshape(tomograms, 1, 2, 1)
    row_scores = jnp.sum(jnp.where(slot_of == slot_ids, returned[..., None], 0.0), axis=(0, 1, 2))
    return (row_scores, reconstruction)


def solution(mesh):
    placed = (
        P("tomo", "ref", None),
        P("tomo"),
        P("tomo"),
        P("tomo"),
        P("tomo", None, None, "ref"),
        P(None, "ref"),
    )
    return jax.shard_map(
        body,
        mesh=mesh,
        in_specs=placed,
        out_specs=(P("tomo"), P("tomo", None, None, "ref")),
        check_vma=False,
    )
```

```python
import numpy as np

import jax
import jax.numpy as jnp
import ml_dtypes
from jax import lax
from jax.experimental import pallas as pl
from jax.experimental.pallas import tpu as pltpu
from jax.sharding import PartitionSpec as P

BOX = 64
HALF = 32
KY_DEV = 4
f32 = jnp.float32
bf16 = jnp.bfloat16


def split_hi_lo(table):
    high = table.astype(np.float32).astype(ml_dtypes.bfloat16)
    low = (table - high.astype(np.float64)).astype(np.float32).astype(ml_dtypes.bfloat16)
    return high, low


def angles(a, b):
    return 2.0 * np.pi / BOX * (np.outer(a, b) % BOX)


def x_table():
    x = np.arange(BOX)
    phase = angles(x, np.arange(HALF))
    real, imag = np.cos(phase), -np.sin(phase)
    imag[:, 0] = np.cos(np.pi * x)
    one = np.concatenate([real, imag, imag, -real], axis=1)
    table = np.zeros((2, BOX, 2, 4 * HALF))
    table[0, :, 0], table[1, :, 1] = one, one
    return np.concatenate(split_hi_lo(table.reshape(2 * BOX, 8 * HALF)), axis=0)


def y_table():
    rows = np.arange(BOX)
    ky = KY_DEV * (rows % 16) + rows // 16
    y = np.concatenate([np.arange(0, BOX, 2), np.arange(1, BOX, 2)])
    cosine, sine = np.cos(angles(ky, y)), np.sin(angles(ky, y))
    zero = np.zeros_like(cosine)
    plain = np.concatenate([cosine, sine], axis=1)
    lower = ky[:, None] < 32
    packed = ky[:, None] % 32 == 0
    real = np.where(lower, np.concatenate([cosine, zero], 1), np.concatenate([zero, cosine], 1))
    imag = np.where(lower, np.concatenate([zero, sine], 1), np.concatenate([-sine, zero], 1))
    real, imag = np.where(packed, plain, real), np.where(packed, plain, imag)
    high, low = split_hi_lo(np.concatenate([plain, real, imag], axis=0))
    return np.concatenate(
        [
            np.concatenate([high, high], axis=1),
            np.concatenate([low, np.zeros_like(low)], axis=1),
        ],
        axis=0,
    )


def z_table():
    phase = angles(np.arange(BOX), np.arange(BOX))
    table = np.zeros((2, BOX, BOX, 2))
    table[0, :, :, 0], table[0, :, :, 1] = np.cos(phase), np.sin(phase)
    table[1, :, :, 0], table[1, :, :, 1] = -np.sin(phase), np.cos(phase)
    return np.concatenate(split_hi_lo(table.reshape(2 * BOX, 2 * BOX)), axis=1)


def reverse_table():
    reverse = np.zeros((2, BOX, 2, BOX))
    for kz in range(BOX):
        reverse[0, kz, 0, -kz % BOX], reverse[1, kz, 1, -kz % BOX] = 1.0, -1.0
    return reverse.reshape(2 * BOX, 2 * BOX).astype(ml_dtypes.bfloat16)


def unfold_table(j):
    own, mirror = np.zeros((KY_DEV, HALF, KY_DEV, BOX)), np.zeros((KY_DEV, HALF, KY_DEV, BOX))
    own_turned, mirror_turned = np.zeros_like(own), np.zeros_like(own)
    here, there = (0, HALF) if j < 8 else (HALF, 0)
    for kyl in range(KY_DEV):
        to = (KY_DEV - kyl) % KY_DEV
        if kyl == 0 and j % 8 == 0:
            own[0, 0, 0, 0] = mirror[0, 0, 0, 0] = 0.5
            own_turned[0, 0, 0, HALF], mirror_turned[0, 0, 0, HALF] = 0.5, -0.5
        else:
            own[kyl, 0, kyl, here] = mirror[kyl, 0, to, there] = 1.0
        for kx in range(1, HALF):
            own[kyl, kx, kyl, kx] = mirror[kyl, kx, to, BOX - kx] = 1.0
    stacked = np.concatenate([own, own, mirror, own_turned, own_turned, mirror_turned], axis=0)
    return stacked.reshape(6 * 2 * BOX, 4 * BOX).astype(ml_dtypes.bfloat16)


def table_of_device():
    j = lax.axis_index("ref")
    kind = jnp.where(j % 8 == 0, 2, 0) + jnp.where(j < 8, 0, 1)
    kinds = jnp.asarray(np.stack([unfold_table(k) for k in (1, 9, 0, 8)]))
    return lax.dynamic_index_in_dim(kinds, kind, keepdims=False)


def params(mebibytes=40):
    return pltpu.CompilerParams(vmem_limit_bytes=mebibytes * 2**20)


def cost(microseconds):
    return pl.CostEstimate(
        flops=0, bytes_accessed=int(microseconds * 3.0e6), transcendentals=0
    )


def dot(a, b):
    return jnp.dot(a, b, preferred_element_type=f32)


def planes_kernel(x_ref, table_ref, out_ref, rows_buf, turn_buf):
    lane = lax.broadcasted_iota(jnp.int32, (1, 128), 1)
    low_half = lane < 64
    even = lane % 64 < 32
    wide_lane = lax.broadcasted_iota(jnp.int32, (1, 256), 1) % 64
    group = x_ref.shape[0]
    for row in range(group):
        volume = x_ref[row].astype(f32)
        for yt in range(32):
            start = 256 * row + 8 * yt
            rows_buf[start : start + 4, :] = volume[:, yt * 128 : (yt + 1) * 128]
    x = jnp.concatenate(
        [
            rows_buf[pl.ds(256 * row + zl, 32, stride=8), :]
            for row in range(group)
            for zl in range(4)
        ],
        axis=0,
    ).astype(bf16)
    along = dot(jnp.concatenate([x, x], axis=1), table_ref[:256])
    for row in range(group):
        tiles = []
        for zp in range(2):
            first, second = [], []
            start = 128 * row + 64 * zp
            for h in range(2):
                a = along[start : start + 32, 128 * h : 128 * h + 128]
                b = along[start + 32 : start + 64, 128 * h : 128 * h + 128]
                first.append(jnp.where(low_half, a, pltpu.roll(b, 64, 1)))
                second.append(jnp.where(low_half, pltpu.roll(a, 64, 1), b))
            tiles.append(jnp.concatenate(first + second, axis=0))
        wide = jnp.concatenate(tiles, axis=1)
        high = wide.astype(bf16)
        low = (wide - high.astype(f32)).astype(bf16)
        full = dot(table_ref[256:], jnp.concatenate([high, low], axis=0))
        full = full[:192] + full[192:]
        planes = jnp.where(wide_lane == 0, full[64:128], full[:64])
        planes = jnp.where(wide_lane == 32, full[128:], planes)
        for zp in range(2):
            i0, i1, i2, i3 = (
                planes[16 * k : 16 * k + 16, 128 * zp : 128 * zp + 128] for k in range(4)
            )
            p0 = jnp.where(low_half, i0, pltpu.roll(i2, 64, 1))
            p2 = jnp.where(low_half, pltpu.roll(i0, 64, 1), i2)
            p1 = jnp.where(low_half, i1, pltpu.roll(i3, 64, 1))
            p3 = jnp.where(low_half, pltpu.roll(i1, 64, 1), i3)
            turned = (
                jnp.where(even, p0, pltpu.roll(p1, 32, 1)),
                jnp.where(even, pltpu.roll(p0, 96, 1), p1),
                jnp.where(even, p2, pltpu.roll(p3, 32, 1)),
                jnp.where(even, pltpu.roll(p2, 96, 1), p3),
            )
            for g in range(4):
                start = 128 * row + (4 * zp + g) * 16
                turn_buf[start : start + 16, :] = turned[g]
    for pair in range(group // 2):
        for j in range(16):
            both = [turn_buf[pl.ds(128 * (2 * pair + e) + j, 8, stride=16), :] for e in range(2)]
            out_ref[j, pair] = jnp.concatenate(both, axis=0).astype(bf16)


def half_planes(particles):
    rows = particles.shape[0]
    group = 16
    return pl.pallas_call(
        planes_kernel,
        grid=(rows // group,),
        in_specs=[
            pl.BlockSpec((group, 4, BOX * BOX), lambda i: (i, 0, 0)),
            pl.BlockSpec((640, 256), lambda i: (0, 0)),
        ],
        out_specs=pl.BlockSpec((16, group // 2, 16, 128), lambda i: (0, i, 0, 0)),
        out_shape=jax.ShapeDtypeStruct((16, rows // 2, 16, 128), bf16),
        scratch_shapes=[
            pltpu.VMEM((group * 256, 128), f32),
            pltpu.VMEM((group * 128, 128), f32),
        ],
        compiler_params=params(58),
        cost_estimate=cost(8.0),
        name="half_planes",
    )(particles, jnp.asarray(np.concatenate([x_table(), y_table()], axis=0)))


def depth_kernel(slot_ref, index_ref, b_ref, table_ref, weight_ref, send_ref, *scratch):
    spec_buf, extra_buf, packed_buf, sems = scratch
    slots = extra_buf.shape[0]
    tomograms = slots // 2
    together = 16
    line = lax.broadcasted_iota(jnp.int32, (4, 128), 0)
    extra_buf[...] = jnp.zeros_like(extra_buf)
    weight = jnp.concatenate([weight_ref[...], weight_ref[...]], axis=0)

    def routed(row):
        slot = slot_ref[row]
        target = send_ref.at[slot // 2, pl.ds(16 * (slot % 2), 16)]
        return slot, pltpu.make_async_copy(spec_buf.at[row], target, sems.at[row])

    def step(i, _):
        done = []
        for p in range(together):
            block = b_ref[:, together * i + p].astype(f32)
            a = block[:, :8, :].reshape(128, 128)
            b = block[:, 8:, :].reshape(128, 128)
            pencils = jnp.concatenate([a, b], axis=1).astype(bf16)
            exact = dot(table_ref[:128], jnp.concatenate([pencils, pencils], axis=0))
            spectra = exact.astype(bf16)
            turned = dot(table_ref[128:, :128], spectra)
            for e in range(2):
                row = 2 * (together * i + p) + e
                one = exact[:, 128 * e : 128 * e + 128]
                spec_buf[row] = one.reshape(16, 8, 128).astype(bf16)
                terms = turned[:, 128 * e : 128 * e + 128] * weight
                value = spectra[:, 128 * e : 128 * e + 128].astype(f32)
                cross = jnp.sum(value * terms, axis=0, keepdims=True)
                high = cross.astype(bf16).astype(f32)
                middle = (cross - high).astype(bf16).astype(f32)
                low = cross - high - middle
                number = (index_ref[row] + 1).astype(f32)
                extra = jnp.where(line == 0, high, jnp.where(line == 1, middle, low))
                extra = jnp.where(line == 3, number, extra)
                done.append(extra)

        for r in range(2 * together):
            slot, copy = routed(2 * together * i + r)

            @pl.when(slot < slots)
            def _():
                copy.start()
                extra_buf[slot] = done[r]

        return 0

    lax.fori_loop(0, b_ref.shape[1] // together, step, 0)

    for t in range(tomograms):
        both = jnp.concatenate([extra_buf[2 * t], extra_buf[2 * t + 1]], axis=0)
        packed_buf[t] = both.astype(bf16)
    last = pltpu.make_async_copy(packed_buf, send_ref.at[:, 32], sems.at[sems.shape[0] - 1])
    last.start()

    def finish(row, _):
        slot, copy = routed(row)

        @pl.when(slot < slots)
        def _():
            copy.wait()

        return 0

    lax.fori_loop(0, 2 * b_ref.shape[1], finish, 0)
    last.wait()


def half_spectra(slot_of, ref_index, pencils, weights, slots):
    vmem = pl.BlockSpec(memory_space=pltpu.VMEM)
    smem = pl.BlockSpec(memory_space=pltpu.SMEM)
    rows = 2 * pencils.shape[1]
    reverse = np.concatenate([reverse_table(), np.zeros_like(reverse_table())], axis=1)
    return pl.pallas_call(
        depth_kernel,
        in_specs=[smem, smem, vmem, vmem, vmem],
        out_specs=pl.BlockSpec(memory_space=pl.ANY),
        out_shape=jax.ShapeDtypeStruct((slots // 2, 33, 8, 128), bf16),
        scratch_shapes=[
            pltpu.VMEM((rows, 16, 8, 128), bf16),
            pltpu.VMEM((slots, 4, 128), f32),
            pltpu.VMEM((slots // 2, 8, 128), bf16),
            pltpu.SemaphoreType.DMA((rows + 1,)),
        ],
        compiler_params=params(52),
        cost_estimate=cost(4.0),
        name="half_spectra",
    )(slot_of, ref_index, pencils, jnp.asarray(np.concatenate([z_table(), reverse])), weights)


def match_kernel(spec_ref, coef_ref, weight_ref, out_ref, sums_buf):
    tomograms = spec_ref.shape[0]
    for t in range(tomograms):
        extra = spec_ref[t, 32].astype(f32)
        for k in range(2):
            slot = 2 * t + k
            value = spec_ref[t, 16 * k : 16 * k + 16].astype(f32).reshape(128, 128)
            index = jnp.maximum(extra[4 * k + 3, 0].astype(jnp.int32) - 1, 0)
            product = value * coef_ref[index]
            squares = jnp.sum(value * value * weight_ref[...], axis=0, keepdims=True)
            parts = jnp.sum(extra[4 * k : 4 * k + 3], axis=0, keepdims=True)
            row = 2 * tomograms + slot
            sums_buf[slot : slot + 1, :] = jnp.sum(product, axis=0, keepdims=True)
            sums_buf[row : row + 1, :] = squares + parts
    totals = jnp.sum(sums_buf[...].T, axis=0, keepdims=True)
    out_ref[...] = jnp.broadcast_to(totals[None], out_ref.shape)


def match(arrived, coefficients, weights):
    slots = 2 * arrived.shape[0]
    vmem = pl.BlockSpec(memory_space=pltpu.VMEM)
    return pl.pallas_call(
        match_kernel,
        in_specs=[vmem, vmem, vmem],
        out_specs=vmem,
        out_shape=jax.ShapeDtypeStruct((16, 1, 2 * slots), f32),
        scratch_shapes=[pltpu.VMEM((2 * slots, 128), f32)],
        compiler_params=params(),
        cost_estimate=cost(2.0),
        name="match",
    )(arrived, coefficients, weights)


def insert_kernel(index_ref, gain_ref, spec_ref, out_ref, sent_ref):
    group = spec_ref.shape[0]
    step = pl.program_id(0)

    @pl.when(step == 0)
    def _():
        out_ref[...] = jnp.zeros_like(out_ref)

    for t in range(group):
        for k in range(2):
            slot = step * 2 * group + 2 * t + k
            value = spec_ref[t, 16 * k : 16 * k + 16].astype(f32).reshape(128, 128)
            gain = gain_ref[slot]
            out_ref[index_ref[slot]] += jnp.where(gain > 0.0, gain * value, 0.0)

    @pl.when(step == pl.num_programs(0) - 1)
    def _():
        sent_ref[...] = out_ref[...].astype(bf16)


def insert(index, gain, arrived, refs):
    slots = index.shape[0]
    group = min(16, slots // 2)
    whole = pl.BlockSpec((refs, 128, 128), lambda i, *_: (0, 0, 0))
    return pl.pallas_call(
        insert_kernel,
        grid_spec=pltpu.PrefetchScalarGridSpec(
            num_scalar_prefetch=2,
            grid=(slots // 2 // group,),
            in_specs=[pl.BlockSpec((group, 33, 8, 128), lambda i, *_: (i, 0, 0, 0))],
            out_specs=[whole, whole],
        ),
        out_shape=[
            jax.ShapeDtypeStruct((refs, 128, 128), f32),
            jax.ShapeDtypeStruct((refs, 128, 128), bf16),
        ],
        compiler_params=params(),
        cost_estimate=cost(25.0),
        name="insert",
    )(index, gain, arrived)


def unfold_kernel(own_ref, near_ref, far_ref, q_ref, reverse_ref, out_ref):
    lane = lax.broadcasted_iota(jnp.int32, (1, 128), 1)
    own = own_ref[...]
    partner = jnp.where(lane < HALF, near_ref[...].astype(f32), far_ref[...].astype(f32)).astype(bf16)
    conjugate = dot(reverse_ref[...], partner)

    def turned(v):
        return jnp.concatenate([v[64:], -v[:64]], axis=0)

    high = own.astype(bf16).astype(f32)
    parts = [high, own - high, conjugate]
    parts = parts + [turned(v) for v in parts]
    full = dot(jnp.concatenate(parts, axis=1).astype(bf16), q_ref[...])
    for lt in range(2):
        for c in range(2):
            out_ref[pl.ds(2 * lt + c, 64, stride=4), :] = full[
                64 * c : 64 * c + 64, 128 * lt : 128 * lt + 128
            ]


def unfold(own, near, far, table):
    refs = own.shape[0]
    one = pl.BlockSpec((None, 128, 128), lambda i: (i, 0, 0))
    packed = pl.pallas_call(
        unfold_kernel,
        grid=(refs,),
        in_specs=[
            one,
            one,
            one,
            pl.BlockSpec((768, 256), lambda i: (0, 0)),
            pl.BlockSpec((128, 128), lambda i: (0, 0)),
        ],
        out_specs=pl.BlockSpec((None, 256, 128), lambda i: (i, 0, 0)),
        out_shape=jax.ShapeDtypeStruct((refs, 256, 128), f32),
        compiler_params=params(),
        cost_estimate=cost(0.5),
        name="unfold",
    )(own, near, far, table, jnp.asarray(reverse_table()))
    tiles = packed.reshape(refs, BOX, 2, 2, 128)
    return tiles.transpose(0, 1, 3, 2, 4).reshape(refs, BOX, 2, 256)


def to_far(values):
    return lax.ppermute(values, "ref", [(j, 15 - j) for j in range(16)])


def to_near(values):
    return lax.ppermute(values, "ref", [(j, -j % 16) for j in range(16)])


def mirrored(values, ky_axis):
    near = to_near(lax.slice_in_dim(values, 0, 1, axis=ky_axis))
    far = to_far(lax.slice_in_dim(values, 1, KY_DEV, axis=ky_axis))
    return jnp.concatenate([near, lax.rev(far, (ky_axis,))], axis=ky_axis)


def minus_index(values, axis):
    return jnp.roll(lax.rev(values, (axis,)), 1, axis)


def minus_kx(values):
    order = np.zeros((BOX, BOX), np.float32)
    for kx in range(BOX):
        order[-kx % BOX, kx] = 1.0
    return jnp.einsum(
        "...x,xk->...k", values, jnp.asarray(order, values.dtype), precision=lax.Precision.HIGHEST,
        preferred_element_type=f32,
    )


def column_kinds():
    j = lax.axis_index("ref")
    return j < 8, (j % 8 == 0) & (jnp.arange(KY_DEV) == 0)


def folded_references(references, spectral_weight):
    refs = references.shape[0]
    weighted = (spectral_weight[None, :, None, :] * references.astype(f32)).astype(bf16)
    weighted = weighted.reshape(refs, BOX, 2, KY_DEV, BOX)
    other = minus_kx(minus_index(mirrored(weighted, 3), 1))
    weighted = weighted.astype(f32)
    real = weighted[:, :, 0] + other[:, :, 0]
    imag = weighted[:, :, 1] - other[:, :, 1]
    real_0, real_32 = real[..., 0], real[..., HALF]
    imag_0, imag_32 = imag[..., 0], imag[..., HALF]
    lower, packed = column_kinds()
    real_end = jnp.where(lower, real_0, real_32)
    real_end = jnp.where(packed, 0.5 * (real_0 - imag_32), real_end)
    imag_end = jnp.where(lower, imag_0, imag_32)
    imag_end = jnp.where(packed, 0.5 * (imag_0 + real_32), imag_end)
    first = jnp.arange(HALF) == 0
    real_half = jnp.where(first, real_end[..., None], real[..., :HALF])
    imag_half = jnp.where(first, imag_end[..., None], imag[..., :HALF])
    both = jnp.stack([real_half, imag_half], axis=1)
    return both.reshape(refs, 128, 128)


def product_weights(spectral_weight):
    ends = spectral_weight[:, : HALF + 1 : HALF]
    ends = ends + minus_index(ends, 0)
    _, packed = column_kinds()
    cross = jnp.where(packed[0], 0.25 * (ends[:, :1] - ends[:, 1:]), 0.0)
    return jnp.where(jnp.arange(128) == 0, cross, 0.0)


def square_weights(spectral_weight):
    near, far = to_near(spectral_weight), to_far(spectral_weight)
    partner = jnp.where(jnp.arange(4 * BOX) < BOX, near, far)
    order, depth = np.zeros((KY_DEV, BOX, KY_DEV, BOX), np.float32), np.zeros((BOX, BOX), np.float32)
    for k in range(BOX):
        depth[k, -k % BOX] = 1.0
        for kyl in range(KY_DEV):
            order[kyl, -k % BOX, -kyl % KY_DEV, k] = 1.0
    highest = lax.Precision.HIGHEST
    other = jnp.dot(jnp.asarray(depth), partner, precision=highest)
    other = jnp.dot(other, jnp.asarray(order.reshape(256, 256)), precision=highest)
    fold = (spectral_weight + other).reshape(BOX, KY_DEV, BOX)
    fold_0, fold_32 = fold[..., 0], fold[..., HALF]
    lower, packed = column_kinds()
    end = jnp.where(packed, 0.25 * (fold_0 + fold_32), jnp.where(lower, fold_0, fold_32))
    first = jnp.arange(HALF) == 0
    squares = jnp.where(first, end[..., None], fold[..., :HALF]).reshape(BOX, 128)
    return jnp.tile(squares, (2, 1))


def body(particles, counts, block_of, ref_index, references, spectral_weight):
    tomograms = lax.axis_size("tomo")
    rows = particles.shape[0]
    slots = 2 * tomograms
    refs = references.shape[0]
    positions = jnp.arange(rows, dtype=jnp.int32)

    is_live = positions < counts[0]
    same = (block_of[:, None] == block_of[None, :]) & is_live[:, None]
    before = positions[:, None] < positions[None, :]
    rank = jnp.sum((same & before).astype(jnp.int32), axis=0)
    slot_of = jnp.where(is_live, 2 * block_of + rank, slots)

    planes = half_planes(particles)
    pencils = lax.all_to_all(planes, "ref", split_axis=0, concat_axis=0, tiled=True)
    outgoing = half_spectra(
        slot_of, ref_index, pencils, product_weights(spectral_weight), slots
    )
    arrived = lax.all_to_all(outgoing, "tomo", split_axis=0, concat_axis=0, tiled=True)
    coefficients, table = lax.optimization_barrier(
        (folded_references(references, spectral_weight), table_of_device())
    )

    numbers = arrived[:, 32, 3::4, 0].reshape(slots)
    slot_index = numbers.astype(jnp.int32) - 1
    filled = slot_index >= 0
    slot_index = jnp.maximum(slot_index, 0)
    spread = match(arrived, coefficients, square_weights(spectral_weight))
    gathered = lax.all_to_all(spread, "ref", split_axis=0, concat_axis=0, tiled=True)
    totals = jnp.sum(gathered, axis=(0, 1)).reshape(2, slots)
    particle_norm = jnp.sqrt(totals[1] / float(BOX) ** 3 + 1e-05)
    slot_scores = jnp.where(filled, totals[0] / (float(BOX) ** 1.5 * particle_norm), 0.0)
    gain = jnp.where(filled, jax.nn.sigmoid(slot_scores) / particle_norm, 0.0)
    gain = gain.astype(bf16).astype(f32)

    sent_scores = jnp.broadcast_to(jnp.pad(slot_scores, (0, 128 - slots))[None, None, :], (tomograms, 8, 128))
    returned = lax.all_to_all(sent_scores, "tomo", split_axis=0, concat_axis=0, tiled=True)
    half, half_sent = insert(slot_index, gain, arrived, refs)
    reconstruction = unfold(half, to_near(half_sent), to_far(half_sent), table)
    returned, reconstruction = lax.optimization_barrier((returned, reconstruction))

    lane = jnp.arange(128, dtype=jnp.int32) - 2 * lax.axis_index("tomo")
    owner = jnp.arange(tomograms, dtype=jnp.int32)[:, None, None]
    slot_ids = jnp.where((lane >= 0) & (lane < 2), 2 * owner + lane, -1)
    row_scores = jnp.sum(
        jnp.where(slot_of[:, None, None] == slot_ids[:, 0][None], returned[:, 0][None], 0.0), axis=(1, 2)
    )
    return (row_scores, reconstruction)


def solution(mesh):
    placed = (
        P("tomo", "ref", None),
        P("tomo"),
        P("tomo"),
        P("tomo"),
        P("tomo", None, None, "ref"),
        P(None, "ref"),
    )
    return jax.shard_map(
        body,
        mesh=mesh,
        in_specs=placed,
        out_specs=(P("tomo"), P("tomo", None, None, "ref")),
        check_vma=False,
    )
```

```python
import numpy as np

import jax
import jax.numpy as jnp
import ml_dtypes
from jax import lax
from jax.experimental import pallas as pl
from jax.experimental.pallas import tpu as pltpu
from jax.sharding import PartitionSpec as P

BOX = 64
HALF = 32
KY_DEV = 4
f32 = jnp.float32
bf16 = jnp.bfloat16


def split_hi_lo(table):
    high = table.astype(np.float32).astype(ml_dtypes.bfloat16)
    low = (table - high.astype(np.float64)).astype(np.float32).astype(ml_dtypes.bfloat16)
    return high, low


def angles(a, b):
    return 2.0 * np.pi / BOX * (np.outer(a, b) % BOX)


def x_table():
    x = np.arange(BOX)
    phase = angles(x, np.arange(HALF))
    real, imag = np.cos(phase), -np.sin(phase)
    imag[:, 0] = np.cos(np.pi * x)
    one = np.concatenate([real, imag, imag, -real], axis=1)
    table = np.zeros((2, BOX, 2, 4 * HALF))
    table[0, :, 0], table[1, :, 1] = one, one
    return np.concatenate(split_hi_lo(table.reshape(2 * BOX, 8 * HALF)), axis=0)


def y_table():
    rows = np.arange(BOX)
    ky = KY_DEV * (rows % 16) + rows // 16
    y = np.concatenate([np.arange(0, BOX, 2), np.arange(1, BOX, 2)])
    cosine, sine = np.cos(angles(ky, y)), np.sin(angles(ky, y))
    zero = np.zeros_like(cosine)
    plain = np.concatenate([cosine, sine], axis=1)
    lower = ky[:, None] < 32
    packed = ky[:, None] % 32 == 0
    real = np.where(lower, np.concatenate([cosine, zero], 1), np.concatenate([zero, cosine], 1))
    imag = np.where(lower, np.concatenate([zero, sine], 1), np.concatenate([-sine, zero], 1))
    real, imag = np.where(packed, plain, real), np.where(packed, plain, imag)
    high, low = split_hi_lo(np.concatenate([plain, real, imag], axis=0))
    return np.concatenate(
        [
            np.concatenate([high, high], axis=1),
            np.concatenate([low, np.zeros_like(low)], axis=1),
        ],
        axis=0,
    )


def z_table():
    phase = angles(np.arange(BOX), np.arange(BOX))
    table = np.zeros((2, BOX, BOX, 2))
    table[0, :, :, 0], table[0, :, :, 1] = np.cos(phase), np.sin(phase)
    table[1, :, :, 0], table[1, :, :, 1] = -np.sin(phase), np.cos(phase)
    return np.concatenate(split_hi_lo(table.reshape(2 * BOX, 2 * BOX)), axis=1)


def reverse_table():
    reverse = np.zeros((2, BOX, 2, BOX))
    for kz in range(BOX):
        reverse[0, kz, 0, -kz % BOX], reverse[1, kz, 1, -kz % BOX] = 1.0, -1.0
    return reverse.reshape(2 * BOX, 2 * BOX).astype(ml_dtypes.bfloat16)


def unfold_table(j):
    own, mirror = np.zeros((KY_DEV, HALF, KY_DEV, BOX)), np.zeros((KY_DEV, HALF, KY_DEV, BOX))
    own_turned, mirror_turned = np.zeros_like(own), np.zeros_like(own)
    here, there = (0, HALF) if j < 8 else (HALF, 0)
    for kyl in range(KY_DEV):
        to = (KY_DEV - kyl) % KY_DEV
        if kyl == 0 and j % 8 == 0:
            own[0, 0, 0, 0] = mirror[0, 0, 0, 0] = 0.5
            own_turned[0, 0, 0, HALF], mirror_turned[0, 0, 0, HALF] = 0.5, -0.5
        else:
            own[kyl, 0, kyl, here] = mirror[kyl, 0, to, there] = 1.0
        for kx in range(1, HALF):
            own[kyl, kx, kyl, kx] = mirror[kyl, kx, to, BOX - kx] = 1.0
    stacked = np.concatenate([own, own, mirror, own_turned, own_turned, mirror_turned], axis=0)
    return stacked.reshape(6 * 2 * BOX, 4 * BOX).astype(ml_dtypes.bfloat16)


def table_of_device():
    j = lax.axis_index("ref")
    kind = jnp.where(j % 8 == 0, 2, 0) + jnp.where(j < 8, 0, 1)
    kinds = jnp.asarray(np.stack([unfold_table(k) for k in (1, 9, 0, 8)]))
    return lax.dynamic_index_in_dim(kinds, kind, keepdims=False)


def params(mebibytes=40):
    return pltpu.CompilerParams(vmem_limit_bytes=mebibytes * 2**20)


def cost(microseconds):
    return pl.CostEstimate(
        flops=0, bytes_accessed=int(microseconds * 3.0e6), transcendentals=0
    )


def dot(a, b):
    return jnp.dot(a, b, preferred_element_type=f32)


def planes_kernel(x_ref, table_ref, out_ref, rows_buf, turn_buf):
    lane = lax.broadcasted_iota(jnp.int32, (1, 128), 1)
    low_half = lane < 64
    even = lane % 64 < 32
    wide_lane = lax.broadcasted_iota(jnp.int32, (1, 256), 1) % 64
    group = x_ref.shape[0]
    for row in range(group):
        volume = x_ref[row].astype(f32)
        for yt in range(32):
            start = 256 * row + 8 * yt
            rows_buf[start : start + 4, :] = volume[:, yt * 128 : (yt + 1) * 128]
    x = jnp.concatenate(
        [
            rows_buf[pl.ds(256 * row + zl, 32, stride=8), :]
            for row in range(group)
            for zl in range(4)
        ],
        axis=0,
    ).astype(bf16)
    along = dot(jnp.concatenate([x, x], axis=1), table_ref[:256])
    for row in range(group):
        tiles = []
        for zp in range(2):
            first, second = [], []
            start = 128 * row + 64 * zp
            for h in range(2):
                a = along[start : start + 32, 128 * h : 128 * h + 128]
                b = along[start + 32 : start + 64, 128 * h : 128 * h + 128]
                first.append(jnp.where(low_half, a, pltpu.roll(b, 64, 1)))
                second.append(jnp.where(low_half, pltpu.roll(a, 64, 1), b))
            tiles.append(jnp.concatenate(first + second, axis=0))
        wide = jnp.concatenate(tiles, axis=1)
        high = wide.astype(bf16)
        low = (wide - high.astype(f32)).astype(bf16)
        full = dot(table_ref[256:], jnp.concatenate([high, low], axis=0))
        full = full[:192] + full[192:]
        planes = jnp.where(wide_lane == 0, full[64:128], full[:64])
        planes = jnp.where(wide_lane == 32, full[128:], planes)
        for zp in range(2):
            i0, i1, i2, i3 = (
                planes[16 * k : 16 * k + 16, 128 * zp : 128 * zp + 128] for k in range(4)
            )
            p0 = jnp.where(low_half, i0, pltpu.roll(i2, 64, 1))
            p2 = jnp.where(low_half, pltpu.roll(i0, 64, 1), i2)
            p1 = jnp.where(low_half, i1, pltpu.roll(i3, 64, 1))
            p3 = jnp.where(low_half, pltpu.roll(i1, 64, 1), i3)
            turned = (
                jnp.where(even, p0, pltpu.roll(p1, 32, 1)),
                jnp.where(even, pltpu.roll(p0, 96, 1), p1),
                jnp.where(even, p2, pltpu.roll(p3, 32, 1)),
                jnp.where(even, pltpu.roll(p2, 96, 1), p3),
            )
            for g in range(4):
                start = 128 * row + (4 * zp + g) * 16
                turn_buf[start : start + 16, :] = turned[g]
    for pair in range(group // 2):
        for j in range(16):
            both = [turn_buf[pl.ds(128 * (2 * pair + e) + j, 8, stride=16), :] for e in range(2)]
            out_ref[j, pair] = jnp.concatenate(both, axis=0).astype(bf16)


def half_planes(particles):
    rows = particles.shape[0]
    group = 16
    return pl.pallas_call(
        planes_kernel,
        grid=(rows // group,),
        in_specs=[
            pl.BlockSpec((group, 4, BOX * BOX), lambda i: (i, 0, 0)),
            pl.BlockSpec((640, 256), lambda i: (0, 0)),
        ],
        out_specs=pl.BlockSpec((16, group // 2, 16, 128), lambda i: (0, i, 0, 0)),
        out_shape=jax.ShapeDtypeStruct((16, rows // 2, 16, 128), bf16),
        scratch_shapes=[
            pltpu.VMEM((group * 256, 128), f32),
            pltpu.VMEM((group * 128, 128), f32),
        ],
        compiler_params=params(58),
        cost_estimate=cost(8.0),
        name="half_planes",
    )(particles, jnp.asarray(np.concatenate([x_table(), y_table()], axis=0)))


def depth_kernel(slot_ref, index_ref, b_ref, table_ref, weight_ref, send_ref, *scratch):
    spec_buf, extra_buf, packed_buf, sems = scratch
    slots = extra_buf.shape[0]
    tomograms = slots // 2
    together = 16
    line = lax.broadcasted_iota(jnp.int32, (4, 128), 0)
    extra_buf[...] = jnp.zeros_like(extra_buf)
    weight = jnp.concatenate([weight_ref[...], weight_ref[...]], axis=0)

    def routed(row):
        slot = slot_ref[row]
        target = send_ref.at[slot // 2, pl.ds(16 * (slot % 2), 16)]
        return slot, pltpu.make_async_copy(spec_buf.at[row], target, sems.at[row])

    def step(i, _):
        done = []
        for p in range(together):
            block = b_ref[:, together * i + p].astype(f32)
            a = block[:, :8, :].reshape(128, 128)
            b = block[:, 8:, :].reshape(128, 128)
            pencils = jnp.concatenate([a, b], axis=1).astype(bf16)
            exact = dot(table_ref[:128], jnp.concatenate([pencils, pencils], axis=0))
            spectra = exact.astype(bf16)
            turned = dot(table_ref[128:, :128], spectra)
            for e in range(2):
                row = 2 * (together * i + p) + e
                one = exact[:, 128 * e : 128 * e + 128]
                spec_buf[row] = one.reshape(16, 8, 128).astype(bf16)
                terms = turned[:, 128 * e : 128 * e + 128] * weight
                value = spectra[:, 128 * e : 128 * e + 128].astype(f32)
                cross = jnp.sum(value * terms, axis=0, keepdims=True)
                high = cross.astype(bf16).astype(f32)
                middle = (cross - high).astype(bf16).astype(f32)
                low = cross - high - middle
                number = (index_ref[row] + 1).astype(f32)
                extra = jnp.where(line == 0, high, jnp.where(line == 1, middle, low))
                extra = jnp.where(line == 3, number, extra)
                done.append(extra)

        for r in range(2 * together):
            slot, copy = routed(2 * together * i + r)

            @pl.when(slot < slots)
            def _():
                copy.start()
                extra_buf[slot] = done[r]

        return 0

    lax.fori_loop(0, b_ref.shape[1] // together, step, 0)

    for t in range(tomograms):
        both = jnp.concatenate([extra_buf[2 * t], extra_buf[2 * t + 1]], axis=0)
        packed_buf[t] = both.astype(bf16)
    last = pltpu.make_async_copy(packed_buf, send_ref.at[:, 32], sems.at[sems.shape[0] - 1])
    last.start()

    def finish(row, _):
        slot, copy = routed(row)

        @pl.when(slot < slots)
        def _():
            copy.wait()

        return 0

    lax.fori_loop(0, 2 * b_ref.shape[1], finish, 0)
    last.wait()


def half_spectra(slot_of, ref_index, pencils, weights, slots):
    vmem = pl.BlockSpec(memory_space=pltpu.VMEM)
    smem = pl.BlockSpec(memory_space=pltpu.SMEM)
    rows = 2 * pencils.shape[1]
    reverse = np.concatenate([reverse_table(), np.zeros_like(reverse_table())], axis=1)
    return pl.pallas_call(
        depth_kernel,
        in_specs=[smem, smem, vmem, vmem, vmem],
        out_specs=pl.BlockSpec(memory_space=pl.ANY),
        out_shape=jax.ShapeDtypeStruct((slots // 2, 33, 8, 128), bf16),
        scratch_shapes=[
            pltpu.VMEM((rows, 16, 8, 128), bf16),
            pltpu.VMEM((slots, 4, 128), f32),
            pltpu.VMEM((slots // 2, 8, 128), bf16),
            pltpu.SemaphoreType.DMA((rows + 1,)),
        ],
        compiler_params=params(52),
        cost_estimate=cost(4.0),
        name="half_spectra",
    )(slot_of, ref_index, pencils, jnp.asarray(np.concatenate([z_table(), reverse])), weights)


def match_kernel(spec_ref, coef_ref, weight_ref, out_ref, sums_buf):
    tomograms = spec_ref.shape[0]
    for t in range(tomograms):
        extra = spec_ref[t, 32].astype(f32)
        for k in range(2):
            slot = 2 * t + k
            value = spec_ref[t, 16 * k : 16 * k + 16].astype(f32).reshape(128, 128)
            index = jnp.maximum(extra[4 * k + 3, 0].astype(jnp.int32) - 1, 0)
            product = value * coef_ref[index]
            squares = jnp.sum(value * value * weight_ref[...], axis=0, keepdims=True)
            parts = jnp.sum(extra[4 * k : 4 * k + 3], axis=0, keepdims=True)
            row = 2 * tomograms + slot
            sums_buf[slot : slot + 1, :] = jnp.sum(product, axis=0, keepdims=True)
            sums_buf[row : row + 1, :] = squares + parts
    totals = jnp.sum(sums_buf[...].T, axis=0, keepdims=True)
    out_ref[...] = jnp.broadcast_to(totals[None], out_ref.shape)


def match(arrived, coefficients, weights):
    slots = 2 * arrived.shape[0]
    vmem = pl.BlockSpec(memory_space=pltpu.VMEM)
    return pl.pallas_call(
        match_kernel,
        in_specs=[vmem, vmem, vmem],
        out_specs=vmem,
        out_shape=jax.ShapeDtypeStruct((16, 1, 2 * slots), f32),
        scratch_shapes=[pltpu.VMEM((2 * slots, 128), f32)],
        compiler_params=params(),
        cost_estimate=cost(2.0),
        name="match",
    )(arrived, coefficients, weights)


def insert_kernel(index_ref, gain_ref, spec_ref, out_ref, sent_ref):
    group = spec_ref.shape[0]
    step = pl.program_id(0)

    @pl.when(step == 0)
    def _():
        out_ref[...] = jnp.zeros_like(out_ref)

    for t in range(group):
        for k in range(2):
            slot = step * 2 * group + 2 * t + k
            value = spec_ref[t, 16 * k : 16 * k + 16].astype(f32).reshape(128, 128)
            gain = gain_ref[slot]
            out_ref[index_ref[slot]] += jnp.where(gain > 0.0, gain * value, 0.0)

    @pl.when(step == pl.num_programs(0) - 1)
    def _():
        sent_ref[...] = out_ref[...].astype(bf16)


def insert(index, gain, arrived, refs):
    slots = index.shape[0]
    group = min(32, slots // 2)
    whole = pl.BlockSpec((refs, 128, 128), lambda i, *_: (0, 0, 0))
    return pl.pallas_call(
        insert_kernel,
        grid_spec=pltpu.PrefetchScalarGridSpec(
            num_scalar_prefetch=2,
            grid=(slots // 2 // group,),
            in_specs=[pl.BlockSpec((group, 33, 8, 128), lambda i, *_: (i, 0, 0, 0))],
            out_specs=[whole, whole],
        ),
        out_shape=[
            jax.ShapeDtypeStruct((refs, 128, 128), f32),
            jax.ShapeDtypeStruct((refs, 128, 128), bf16),
        ],
        compiler_params=params(),
        cost_estimate=cost(25.0),
        name="insert",
    )(index, gain, arrived)


def unfold_kernel(own_ref, near_ref, far_ref, q_ref, reverse_ref, out_ref):
    lane = lax.broadcasted_iota(jnp.int32, (1, 128), 1)
    own = own_ref[...]
    partner = jnp.where(lane < HALF, near_ref[...].astype(f32), far_ref[...].astype(f32)).astype(bf16)
    conjugate = dot(reverse_ref[...], partner)

    def turned(v):
        return jnp.concatenate([v[64:], -v[:64]], axis=0)

    high = own.astype(bf16).astype(f32)
    parts = [high, own - high, conjugate]
    parts = parts + [turned(v) for v in parts]
    full = dot(jnp.concatenate(parts, axis=1).astype(bf16), q_ref[...])
    for lt in range(2):
        for c in range(2):
            out_ref[pl.ds(2 * lt + c, 64, stride=4), :] = full[
                64 * c : 64 * c + 64, 128 * lt : 128 * lt + 128
            ]


def unfold(own, near, far, table):
    refs = own.shape[0]
    one = pl.BlockSpec((None, 128, 128), lambda i: (i, 0, 0))
    packed = pl.pallas_call(
        unfold_kernel,
        grid=(refs,),
        in_specs=[
            one,
            one,
            one,
            pl.BlockSpec((768, 256), lambda i: (0, 0)),
            pl.BlockSpec((128, 128), lambda i: (0, 0)),
        ],
        out_specs=pl.BlockSpec((None, 256, 128), lambda i: (i, 0, 0)),
        out_shape=jax.ShapeDtypeStruct((refs, 256, 128), f32),
        compiler_params=params(),
        cost_estimate=cost(0.5),
        name="unfold",
    )(own, near, far, table, jnp.asarray(reverse_table()))
    tiles = packed.reshape(refs, BOX, 2, 2, 128)
    return tiles.transpose(0, 1, 3, 2, 4).reshape(refs, BOX, 2, 256)


def to_far(values):
    return lax.ppermute(values, "ref", [(j, 15 - j) for j in range(16)])


def to_near(values):
    return lax.ppermute(values, "ref", [(j, -j % 16) for j in range(16)])


def mirrored(values, ky_axis):
    near = to_near(lax.slice_in_dim(values, 0, 1, axis=ky_axis))
    far = to_far(lax.slice_in_dim(values, 1, KY_DEV, axis=ky_axis))
    return jnp.concatenate([near, lax.rev(far, (ky_axis,))], axis=ky_axis)


def minus_index(values, axis):
    return jnp.roll(lax.rev(values, (axis,)), 1, axis)


def minus_kx(values):
    order = np.zeros((BOX, BOX), np.float32)
    for kx in range(BOX):
        order[-kx % BOX, kx] = 1.0
    return jnp.einsum(
        "...x,xk->...k", values, jnp.asarray(order, values.dtype), precision=lax.Precision.HIGHEST,
        preferred_element_type=f32,
    )


def column_kinds():
    j = lax.axis_index("ref")
    return j < 8, (j % 8 == 0) & (jnp.arange(KY_DEV) == 0)


def folded_references(references, spectral_weight):
    refs = references.shape[0]
    weighted = (spectral_weight[None, :, None, :] * references.astype(f32)).astype(bf16)
    weighted = weighted.reshape(refs, BOX, 2, KY_DEV, BOX)
    other = minus_kx(minus_index(mirrored(weighted, 3), 1))
    weighted = weighted.astype(f32)
    real = weighted[:, :, 0] + other[:, :, 0]
    imag = weighted[:, :, 1] - other[:, :, 1]
    real_0, real_32 = real[..., 0], real[..., HALF]
    imag_0, imag_32 = imag[..., 0], imag[..., HALF]
    lower, packed = column_kinds()
    real_end = jnp.where(lower, real_0, real_32)
    real_end = jnp.where(packed, 0.5 * (real_0 - imag_32), real_end)
    imag_end = jnp.where(lower, imag_0, imag_32)
    imag_end = jnp.where(packed, 0.5 * (imag_0 + real_32), imag_end)
    first = jnp.arange(HALF) == 0
    real_half = jnp.where(first, real_end[..., None], real[..., :HALF])
    imag_half = jnp.where(first, imag_end[..., None], imag[..., :HALF])
    both = jnp.stack([real_half, imag_half], axis=1)
    return both.reshape(refs, 128, 128)


def product_weights(spectral_weight):
    ends = spectral_weight[:, : HALF + 1 : HALF]
    ends = ends + minus_index(ends, 0)
    _, packed = column_kinds()
    cross = jnp.where(packed[0], 0.25 * (ends[:, :1] - ends[:, 1:]), 0.0)
    return jnp.where(jnp.arange(128) == 0, cross, 0.0)


def square_weights(spectral_weight):
    near, far = to_near(spectral_weight), to_far(spectral_weight)
    partner = jnp.where(jnp.arange(4 * BOX) < BOX, near, far)
    order, depth = np.zeros((KY_DEV, BOX, KY_DEV, BOX), np.float32), np.zeros((BOX, BOX), np.float32)
    for k in range(BOX):
        depth[k, -k % BOX] = 1.0
        for kyl in range(KY_DEV):
            order[kyl, -k % BOX, -kyl % KY_DEV, k] = 1.0
    highest = lax.Precision.HIGHEST
    other = jnp.dot(jnp.asarray(depth), partner, precision=highest)
    other = jnp.dot(other, jnp.asarray(order.reshape(256, 256)), precision=highest)
    fold = (spectral_weight + other).reshape(BOX, KY_DEV, BOX)
    fold_0, fold_32 = fold[..., 0], fold[..., HALF]
    lower, packed = column_kinds()
    end = jnp.where(packed, 0.25 * (fold_0 + fold_32), jnp.where(lower, fold_0, fold_32))
    first = jnp.arange(HALF) == 0
    squares = jnp.where(first, end[..., None], fold[..., :HALF]).reshape(BOX, 128)
    return jnp.tile(squares, (2, 1))


def body(particles, counts, block_of, ref_index, references, spectral_weight):
    tomograms = lax.axis_size("tomo")
    rows = particles.shape[0]
    slots = 2 * tomograms
    refs = references.shape[0]
    positions = jnp.arange(rows, dtype=jnp.int32)

    is_live = positions < counts[0]
    same = (block_of[:, None] == block_of[None, :]) & is_live[:, None]
    before = positions[:, None] < positions[None, :]
    rank = jnp.sum((same & before).astype(jnp.int32), axis=0)
    slot_of = jnp.where(is_live, 2 * block_of + rank, slots)

    planes = half_planes(particles)
    pencils = lax.all_to_all(planes, "ref", split_axis=0, concat_axis=0, tiled=True)
    outgoing = half_spectra(
        slot_of, ref_index, pencils, product_weights(spectral_weight), slots
    )
    arrived = lax.all_to_all(outgoing, "tomo", split_axis=0, concat_axis=0, tiled=True)
    coefficients, table = lax.optimization_barrier(
        (folded_references(references, spectral_weight), table_of_device())
    )

    numbers = arrived[:, 32, 3::4, 0].reshape(slots)
    slot_index = numbers.astype(jnp.int32) - 1
    filled = slot_index >= 0
    slot_index = jnp.maximum(slot_index, 0)
    spread = match(arrived, coefficients, square_weights(spectral_weight))
    gathered = lax.all_to_all(spread, "ref", split_axis=0, concat_axis=0, tiled=True)
    totals = jnp.sum(gathered, axis=(0, 1)).reshape(2, slots)
    particle_norm = jnp.sqrt(totals[1] / float(BOX) ** 3 + 1e-05)
    slot_scores = jnp.where(filled, totals[0] / (float(BOX) ** 1.5 * particle_norm), 0.0)
    gain = jnp.where(filled, jax.nn.sigmoid(slot_scores) / particle_norm, 0.0)
    gain = gain.astype(bf16).astype(f32)

    sent_scores = jnp.broadcast_to(jnp.pad(slot_scores, (0, 128 - slots))[None, None, :], (tomograms, 1, 128))
    returned = lax.all_to_all(sent_scores, "tomo", split_axis=0, concat_axis=0, tiled=True)
    half, half_sent = insert(slot_index, gain, arrived, refs)
    reconstruction = unfold(half, to_near(half_sent), to_far(half_sent), table)
    returned, reconstruction = lax.optimization_barrier((returned, reconstruction))

    lane = jnp.arange(128, dtype=jnp.int32) - 2 * lax.axis_index("tomo")
    owner = jnp.arange(tomograms, dtype=jnp.int32)[:, None, None]
    slot_ids = jnp.where((lane >= 0) & (lane < 2), 2 * owner + lane, -1)
    row_scores = jnp.sum(
        jnp.where(slot_of[:, None, None] == slot_ids[:, 0][None], returned[:, 0][None], 0.0), axis=(1, 2)
    )
    return (row_scores, reconstruction)


def solution(mesh):
    placed = (
        P("tomo", "ref", None),
        P("tomo"),
        P("tomo"),
        P("tomo"),
        P("tomo", None, None, "ref"),
        P(None, "ref"),
    )
    return jax.shard_map(
        body,
        mesh=mesh,
        in_specs=placed,
        out_specs=(P("tomo"), P("tomo", None, None, "ref")),
        check_vma=False,
    )
```
